32 devices in a mesh: groups: 2 (over y), expert: 8 (over z, x), section: 2 (over core).
Axes of the slice: x: 2, y: 2, z: 4, core: 2. Of those that a mesh axis runs over, the one named last changes fastest.
Arguments:
- tokens: bfloat16 [2, 128, 7168], P(None, ('groups', 'expert')), parts along dimension 1, may hold values from -6 to 6
- routes: int32 [2, 2, 128, 4], P('section', None, ('groups', 'expert')), parts along dimension 2, may hold values from 0 to 15, all different within a row; in each aligned block of 8 rows (0 to 7, 8 to 15, ..., all dimensions but the last counted through in order) at most 3 rows name the same one
- norm_gain: float32 [2, 7168], P('section'), may hold values from 0.5 to 1.5
- router_weight: bfloat16 [2, 7168, 16], P('section'), may hold values from -0.125 to 0.125
- gate_weight: bfloat16 [2, 7168, 16384], P('section', None, 'expert'), may hold values from -0.0625 to 0.0625
- up_weight: bfloat16 [2, 7168, 16384], P('section', None, 'expert'), may hold values from -0.0625 to 0.0625
- down_weight: bfloat16 [2, 16384, 7168], P('section', 'expert'), may hold values from -0.375 to 0.375
Outputs:
- encoded: bfloat16 [2, 128, 7168], P('section', ('groups', 'expert')), parts along dimension 1
The draws below stay inside these ranges and needn't reach their ends.
There are 2 independent parts, one for each index of `groups`. The reference program is written for one: setup_inputs(seed, part) draws one part's arguments, and reference() takes and returns one part's arrays. A program takes and returns all parts, laid end to end along the dimension named above; an argument that names none is the same for every part. Nothing has to cross between parts.
Inputs may be any that keep to these rules, and one draw needn't show every extreme that they name: `routes`: each token names 4 different experts. For every layer, micro-batch and aligned block of 8 tokens, no expert is named by more than 3 of the block's tokens.
All inputs are finite; a program needn't handle non-finite values.
Results may differ from the reference program's by a relative error of at most 0.0074.
Values may be sent and summed in bfloat16 or wider, within the bound.
No kernel may reach another device: no remote copies, remote signals or barrier semaphores. Data moves between devices by JAX's collectives and lax.ppermute only.
A program may use at most 256 MiB of HBM per device.

```python
import math
import jax
import jax.numpy as jnp
import numpy as np
from jax import lax

D = 7168
FF = 1024
EXPERTS = 16
TOP = 4
TOK_DEV = 8
MB = 2
LAYERS = 2
TOKENS = 64
CAP = 3
N_EXPERT = 8


def level_of(own_key, extent, pieces, least, high):
    def one(dim, parts):
        steps = jax.random.uniform(jax.random.fold_in(jax.random.fold_in(own_key, 6), dim), (parts,), jnp.float32, least / len(pieces), high / len(pieces))
        return jnp.repeat(jnp.exp(steps), extent[dim] // parts).reshape((-1,) + (1,) * (len(extent) - dim - 1))

    gain = one(*pieces[0])
    for cut in pieces[1:]:
        gain = gain * one(*cut)
    return gain


def deal_out(stream_key, own, number, rows, amount, top, reach, lean):
    order = jax.random.permutation(stream_key, amount)
    packed, usual = shares(amount, rows * top, reach, lean, True), shares(amount, rows * top, reach, lean, False)
    places = jnp.arange(amount)

    def named(sizes, turn):
        used = int((sizes > 0).sum())
        fixed = max(1, used // 4)
        shifted = fixed + (places - fixed + turn * (used - fixed)) % max(1, amount - fixed)
        return jnp.zeros((amount,), jnp.int32).at[order[jnp.where(places < fixed, places, shifted)]].set(jnp.asarray(sizes, jnp.int32))

    sizes = jnp.where(number % 4 == 0, named(packed, number // 4), named(usual, number - number // 4 - 1))
    mixed = jax.random.permutation(jax.random.fold_in(own, 3), amount)
    source_of, taker = mixed[0:amount // 2 * 2:2], mixed[1:amount // 2 * 2:2]
    slack = jnp.minimum(sizes[source_of] - 1, reach - sizes[taker]) // 2
    slack = jnp.where((source_of == order[0]) | (taker == order[0]) | (sizes[taker] == 0), 0, jnp.maximum(slack, 0))
    shifted = jax.random.randint(jax.random.fold_in(own, 4), (amount // 2,), 0, 1 << 20) % (slack + 1)
    sizes = sizes.at[source_of].add(-shifted).at[taker].add(shifted)
    labels = jnp.searchsorted(jnp.cumsum(sizes), jnp.arange(rows * top), side="right").astype(jnp.int32)
    grid = labels.reshape(top, rows).T
    grid = grid[jax.random.permutation(jax.random.fold_in(own, 1), rows)]
    turn = jax.random.randint(jax.random.fold_in(own, 2), (rows, 1), 0, top)
    return jnp.take_along_axis(grid, (jnp.arange(top)[None, :] + turn) % top, axis=1)


def shares(amount, total, reach, slope, full):
    weights = [(1 << 20) // math.isqrt(rank ** slope) + 1 for rank in range(1, amount + 1)]
    largest = reach if full else min(reach, max(-(-total // amount), total * weights[0] // sum(weights)))
    least = 1 if total - largest >= amount - 1 else 0
    counts, surplus = [largest] + [least] * (amount - 1), total - largest - least * (amount - 1)
    while surplus > 0:
        candidates = [i for i in range(1, amount) if counts[i] < largest] or [i for i in range(1, amount) if counts[i] < reach]
        whole, left = sum([weights[i] for i in candidates]), surplus
        for i in candidates:
            extra = min(reach - counts[i], max(1, left * weights[i] // whole), surplus)
            counts[i] = counts[i] + extra
            surplus = surplus - extra
    return np.array(counts)


def normal_values(key, shape, spread, most, split=(), kind=jnp.bfloat16):
    array = jax.random.normal(key, shape, jnp.float32) * spread
    if len(split) > 0:
        array = level_of(key, shape, split, -0.22, 0.18) * array
    return jnp.clip(array, min=-most, max=most).astype(kind)


def setup_inputs(seed: int = 0, part: int = 0) -> dict:
    streams_of = jax.random.split(jax.random.key(seed), 8)
    part_keys = jax.random.split(jax.random.fold_in(streams_of[7], part), 8)
    tokens = normal_values(part_keys[0], (MB, TOKENS, D), 1.0, 6.0, ((1, 8),))
    routes_keys = jax.random.split(jax.random.fold_in(part_keys[1], 1), LAYERS * MB * TOKENS // TOK_DEV)
    routes_turns = jax.random.permutation(jax.random.fold_in(part_keys[1], 3), LAYERS * MB * TOKENS // TOK_DEV)
    routes = jax.vmap(lambda own, number: deal_out(jax.random.fold_in(part_keys[1], 2), own, number, TOK_DEV, EXPERTS, TOP, CAP, 2))(routes_keys, routes_turns).reshape((LAYERS, MB, TOKENS, TOP))
    norm_gain = jnp.clip(0.5 + 1.0 * jax.random.uniform(streams_of[2], (LAYERS, D), jnp.float32) ** level_of(streams_of[2], (LAYERS, D), ((0, 2),), -0.2, 0.2), 0.5, 1.5)
    router_weight = normal_values(streams_of[3], (LAYERS, D, EXPERTS), (D // 4) ** -0.5, 0.125, ((0, 2),))
    gate_weight = normal_values(streams_of[4], (LAYERS, D, EXPERTS * FF), D ** -0.5, 0.0625, ((0, 2), (2, 8)))
    up_weight = normal_values(streams_of[5], (LAYERS, D, EXPERTS * FF), D ** -0.5, 0.0625, ((0, 2), (2, 8)))
    down_weight = normal_values(streams_of[6], (LAYERS, EXPERTS * FF, D), (FF // 4) ** -0.5, 0.375, ((0, 2), (1, 8)))
    return {"tokens": tokens, "routes": routes, "norm_gain": norm_gain, "router_weight": router_weight, "gate_weight": gate_weight, "up_weight": up_weight, "down_weight": down_weight}


EPSILON = 1e-06

def moe_layer(token_rows, routes, gain_row, router_weight, gate_weight, up_weight, down_weight):
    micro_count, row_count, model_width = token_rows.shape
    total_rows = micro_count * row_count
    values = token_rows.astype(jnp.float32).reshape(total_rows, model_width)
    factor = lax.rsqrt(lax.optimization_barrier(jnp.mean(values * values, axis=-1, keepdims=True)) + EPSILON)
    normed = (values * factor * gain_row).astype(jnp.bfloat16)
    logits = jnp.dot(normed, router_weight, preferred_element_type=jnp.float32)
    affinity = jax.nn.sigmoid(logits)
    flat_routes = routes.reshape(total_rows, TOP)
    expert_hit = (flat_routes[..., None] == jnp.arange(EXPERTS, dtype=jnp.int32)).astype(jnp.float32)
    picked = lax.optimization_barrier(jnp.sum(expert_hit * affinity[:, None, :], axis=-1))
    gate_vals = picked / lax.optimization_barrier(jnp.sum(picked, axis=-1, keepdims=True))
    expert_gate = lax.optimization_barrier(jnp.sum(expert_hit * gate_vals[..., None], axis=1))
    routed = lax.optimization_barrier(jnp.sum(expert_hit, axis=1))
    row_limit = MB * N_EXPERT * CAP
    shards = max(1, N_EXPERT // EXPERTS)
    unit_width = FF // shards

    def one_expert(expert_idx):
        gate_block = lax.dynamic_slice_in_dim(gate_weight, expert_idx * FF, FF, 1).astype(jnp.float32)
        up_block = lax.dynamic_slice_in_dim(up_weight, expert_idx * FF, FF, 1).astype(jnp.float32)
        down_block = lax.dynamic_slice_in_dim(down_weight, expert_idx * FF, FF, 0).astype(jnp.float32)
        member = routed[:, expert_idx]
        row_index = jnp.nonzero(member > 0, size=row_limit, fill_value=0)[0].astype(jnp.int32)
        live_rows = (jnp.arange(row_limit) < jnp.sum(member)).astype(jnp.float32)
        chosen = normed[row_index].astype(jnp.float32)
        gate_part = jnp.dot(chosen, gate_block)
        up_part = jnp.dot(chosen, up_block)
        hidden = (jax.nn.silu(gate_part) * up_part).astype(jnp.bfloat16)
        hidden = lax.optimization_barrier(hidden).astype(jnp.float32).reshape(row_limit, shards, unit_width)
        partial_value = jnp.einsum('rsf,sfd->rsd', hidden, down_block.reshape(shards, unit_width, model_width))
        partial_value = lax.optimization_barrier(partial_value.astype(jnp.bfloat16)).astype(jnp.float32)
        scale = expert_gate[:, expert_idx][row_index] * live_rows
        weighted_sum = lax.optimization_barrier(jnp.sum(partial_value, axis=1)) * scale[:, None]
        return (row_index, weighted_sum)
    indices, totals = lax.map(one_expert, jnp.arange(EXPERTS, dtype=jnp.int32))
    branch = jnp.zeros((total_rows, model_width), jnp.float32).at[indices.reshape(-1)].add(totals.reshape(-1, model_width))
    return (values + branch).astype(jnp.bfloat16).reshape(micro_count, row_count, model_width)

def reference(tokens, routes, norm_gain, router_weight, gate_weight, up_weight, down_weight):
    hidden_state = tokens
    for layer_idx in range(LAYERS):
        hidden_state = moe_layer(hidden_state, routes[layer_idx], norm_gain[layer_idx], router_weight[layer_idx], gate_weight[layer_idx], up_weight[layer_idx], down_weight[layer_idx])
    return hidden_state
```

```python
import functools

import jax
import jax.numpy as jnp
import numpy as np
from jax import lax
from jax.experimental import pallas as pl
from jax.experimental.pallas import tpu as pltpu
from jax.sharding import PartitionSpec as P

FF = 1024
EXPERTS = 16
EPSILON = 1e-06
CHUNKS = 2
LANES = 128
VMEM_LIMIT = 50 << 20


def bit_orders(count):
    bits = [1 << k for k in range(count.bit_length() - 1)]
    return bits, bits[1:] + bits[:1]


def block_of(order):
    table = [0]
    for bit in reversed(order):
        table = table + [b ^ bit for b in table]
    return table


def swap_tables(count):
    first, second = (block_of(order) for order in bit_orders(count))
    to_second = [second.index(b) for b in first]
    to_first = [first.index(b) for b in second]
    return np.array([to_second, to_first], np.int32)


def exchange(value, level):
    count = lax.axis_size("expert")
    orders = bit_orders(count)
    pairs = [
        (2 * e + s, 2 * (e ^ orders[s][level]) + s) for e in range(count) for s in range(2)
    ]
    return lax.ppermute(value, ("expert", "section"), pairs)


def swap(value):
    return lax.ppermute(value, "section", [(0, 1), (1, 0)])


def add(left, right):
    return left.astype(jnp.float32) + right.astype(jnp.float32)


def spread(value, level):
    while level >= 0:
        value = jnp.concatenate([value, exchange(value, level)], axis=0)
        level -= 1
    return value


def reduce_to(value, last):
    level = 0
    while value.shape[0] > last:
        half = value.shape[0] // 2
        received = exchange(value[half:], level)
        value = add(value[:half], received)
        if half > 1:
            value = value.astype(jnp.bfloat16)
        level += 1
    return value, level


def gate_up_kernel(first, last, width, model_width, tile, meta, *refs):
    refs = list(refs)
    own, other, gain, router, gate_w, up_w = refs[:6]
    refs = refs[6:]
    if not first:
        gate_in, up_in, stats_in = refs[:3]
        refs = refs[3:]
    if last:
        routes, hidden = refs[:2]
        refs = refs[2:]
    else:
        gate_out, up_out, stats_out = refs[:3]
        refs = refs[3:]
    scaled, stats = refs
    count, rows, _ = own.shape
    section = meta[0]
    step = pl.program_id(0)

    @pl.when((meta[1] == 1) & (step == 0))
    def _():
        own_at = pl.multiple_of(section * width, LANES)
        other_at = pl.multiple_of((1 - section) * width, LANES)
        lane = lax.broadcasted_iota(jnp.int32, (rows, LANES), 1)
        own_gain = gain[:, pl.ds(own_at, width)]
        other_gain = gain[:, pl.ds(other_at, width)]
        for p in range(count):
            at = pl.ds(p * rows, rows)
            mine = own[p].astype(jnp.float32)
            theirs = other[meta[3 + p]].astype(jnp.float32)
            scaled[at, pl.ds(own_at, width)] = (mine * own_gain).astype(jnp.bfloat16)
            scaled[at, pl.ds(other_at, width)] = (theirs * other_gain).astype(jnp.bfloat16)
            square = jnp.sum(mine * mine + theirs * theirs, axis=-1, keepdims=True)
            stats[at, :] = jnp.where(lane == EXPERTS, square, 0.0)
        logits = jnp.dot(scaled[...], router[0], preferred_element_type=jnp.float32)
        stats[:, :EXPERTS] = logits
        if not first:
            stats[...] += stats_in[...]
        if not last:
            stats_out[...] = stats[...]
        else:
            values = stats[...]
            all_lane = lax.broadcasted_iota(jnp.int32, values.shape, 1)
            total = jnp.sum(jnp.where(all_lane == EXPERTS, values, 0.0), axis=-1, keepdims=True)
            factor = lax.rsqrt(total / model_width + EPSILON)
            affinity = jax.nn.sigmoid(values * factor)
            named = routes[...].astype(jnp.float32).reshape(values.shape)
            hit = jnp.zeros(values.shape, jnp.bool_)
            for k in range(4):
                hit = hit | (named[:, k : k + 1] == all_lane.astype(jnp.float32))
            picked = jnp.where(hit & (all_lane < EXPERTS), affinity, 0.0)
            gates = picked / jnp.sum(picked, axis=-1, keepdims=True)
            stats[...] = jnp.where(all_lane == EXPERTS, factor, gates)

    @pl.when(meta[1] == 1)
    def _():
        gate_part = jnp.dot(scaled[...], gate_w[0], preferred_element_type=jnp.float32)
        up_part = jnp.dot(scaled[...], up_w[0], preferred_element_type=jnp.float32)
        if not first:
            gate_part += gate_in[...]
            up_part += up_in[...]
        if not last:
            gate_out[...] = gate_part
            up_out[...] = up_part
        else:
            values = stats[...]
            lane = lax.broadcasted_iota(jnp.int32, values.shape, 1)
            expert = (meta[2] + step * tile) // FF
            factor = jnp.sum(jnp.where(lane == EXPERTS, values, 0.0), axis=-1, keepdims=True)
            weight = jnp.sum(jnp.where(lane == expert, values, 0.0), axis=-1, keepdims=True)
            gated = jax.nn.silu(gate_part * factor) * (up_part * (factor * weight))
            hidden[...] = gated.astype(jnp.bfloat16)


def gate_up(meta, own, other, gain, router, gate_w, up_w, carried, routes, chunk):
    count, rows, width = own.shape
    total = count * rows
    model_width, units = gate_w.shape[1:]
    tile = min(256, units)
    first, last = chunk == 0, chunk == CHUNKS - 1
    whole3 = lambda i, m: (0, 0, 0)
    column = pl.BlockSpec((total, tile), lambda i, m: (0, i))
    weight = pl.BlockSpec((1, 2 * width, tile), lambda i, m: (0, chunk, i * m[1]))
    flat = pl.BlockSpec((total, LANES), lambda i, m: (0, 0))
    specs = [
        pl.BlockSpec((count, rows, width), whole3),
        pl.BlockSpec((count, rows, width), whole3),
        pl.BlockSpec((1, 2 * width), lambda i, m: (0, chunk)),
        pl.BlockSpec((1, 2 * width, EXPERTS), lambda i, m: (0, chunk, 0)),
        weight,
        weight,
    ]
    operands = [own, other, gain, router, gate_w, up_w]
    if not first:
        specs += [column, column, flat]
        operands += list(carried)
    if last:
        specs.append(pl.BlockSpec((count, rows, LANES), whole3))
        operands.append(routes)
        out_specs = column
        out_shape = jax.ShapeDtypeStruct((total, units), jnp.bfloat16)
    else:
        out_specs = [column, column, flat]
        out_shape = [
            jax.ShapeDtypeStruct((total, units), jnp.float32),
            jax.ShapeDtypeStruct((total, units), jnp.float32),
            jax.ShapeDtypeStruct((total, LANES), jnp.float32),
        ]
    return pl.pallas_call(
        functools.partial(gate_up_kernel, first, last, width, model_width, tile),
        grid_spec=pltpu.PrefetchScalarGridSpec(
            num_scalar_prefetch=1,
            grid=(units // tile,),
            in_specs=specs,
            out_specs=out_specs,
            scratch_shapes=[
                pltpu.VMEM((total, 2 * width), jnp.bfloat16),
                pltpu.VMEM((total, LANES), jnp.float32),
            ],
        ),
        out_shape=out_shape,
        compiler_params=pltpu.CompilerParams(vmem_limit_bytes=VMEM_LIMIT),
        name="gate_up",
    )(meta, *operands)


def down_kernel(half_steps, meta, hidden, down_w, other_out, own_out):
    count, rows, _ = own_out.shape
    step = pl.program_id(0)

    @pl.when(meta[1] == 1)
    def _():
        part = jnp.dot(hidden[...], down_w[0], preferred_element_type=jnp.float32)
        part = part.astype(jnp.bfloat16)

        @pl.when(step < half_steps)
        def _():
            for p in range(count):
                other_out[meta[3 + p]] = part[p * rows : (p + 1) * rows]

        @pl.when(step >= half_steps)
        def _():
            for p in range(count):
                own_out[p] = part[p * rows : (p + 1) * rows]


def down(meta, hidden, down_w, count, chunk):
    total, units = hidden.shape
    model_width = down_w.shape[2]
    width = model_width // (2 * CHUNKS)
    rows = total // count
    tile = width // 2 if width % (2 * LANES) == 0 else width
    steps = width // tile

    def column(i, m):
        side = jnp.where(i < steps, 1 - m[0], m[0])
        return (2 * chunk + side) * steps + jnp.where(i < steps, i, i - steps)

    shape = jax.ShapeDtypeStruct((count, rows, width), jnp.bfloat16)
    return pl.pallas_call(
        functools.partial(down_kernel, steps),
        grid_spec=pltpu.PrefetchScalarGridSpec(
            num_scalar_prefetch=1,
            grid=(2 * steps,),
            in_specs=[
                pl.BlockSpec((total, units), lambda i, m: (0, 0)),
                pl.BlockSpec((1, units, tile), lambda i, m: (0, 0, column(i * m[1], m))),
            ],
            out_specs=[
                pl.BlockSpec((count, rows, tile), lambda i, m: (0, 0, jnp.minimum(i, steps - 1))),
                pl.BlockSpec((count, rows, tile), lambda i, m: (0, 0, jnp.maximum(i - steps, 0))),
            ],
        ),
        out_shape=[shape, shape],
        compiler_params=pltpu.CompilerParams(vmem_limit_bytes=VMEM_LIMIT),
        name="down",
    )(meta, hidden, down_w)


def local(tokens, routes, norm_gain, router_weight, gate_weight, up_weight, down_weight):
    count = lax.axis_size("expert")
    micro, rows, model_width = tokens.shape
    block = micro * rows
    width = model_width // (2 * CHUNKS)
    top = routes.shape[-1]
    units = gate_weight.shape[-1]
    section = lax.axis_index("section")
    first = section == 0
    deepest = count.bit_length() - 2
    tables = jnp.asarray(swap_tables(count))
    table = jnp.where(first, tables[0], tables[1])

    def meta_of(layer):
        head = jnp.stack(
            [section, (section == layer).astype(jnp.int32), lax.axis_index("expert") * units]
        )
        return jnp.concatenate([head.astype(jnp.int32), table])

    def layer_hidden(meta, pieces, named):
        carried = None
        for c, (own, other) in enumerate(pieces):
            carried = gate_up(
                meta, own, other, norm_gain, router_weight, gate_weight, up_weight, carried, named, c
            )
        return carried

    def layer_partial(meta, hidden, layer, c):
        other, own = down(meta, hidden, down_weight, count, c)
        return jnp.where(section == layer, own, swap(other))

    parts = tokens.reshape(block, CHUNKS, 2, width)
    mine = jnp.where(first, parts[:, :, 0], parts[:, :, 1])
    named = jnp.pad(
        routes.reshape(block, top).astype(jnp.bfloat16), ((0, 0), (0, LANES - top))
    )
    pieces = []
    for c in range(CHUNKS):
        value = mine[:, c]
        if c == 0:
            value = jnp.concatenate([value, named], axis=-1)
        value = spread(value[None], deepest)
        if c == 0:
            all_named = value[:, :, width:]
            value = value[:, :, :width]
        pieces.append((value, swap(value)))

    meta = meta_of(0)
    hidden = layer_hidden(meta, pieces, all_named)
    after = []
    for c in range(CHUNKS):
        value = layer_partial(meta, hidden, 0, c)
        value, level = reduce_to(value, 2)
        value = value.astype(jnp.bfloat16)
        received = exchange(value, level)
        value = add(value, jnp.flip(received, axis=0))
        value = (pieces[c][0][:2].astype(jnp.float32) + value).astype(jnp.bfloat16)
        value = spread(value, level - 1)
        after.append((value, swap(value)))

    meta = meta_of(1)
    hidden = layer_hidden(meta, after, all_named)
    results = []
    for c in range(CHUNKS):
        value = layer_partial(meta, hidden, 1, c)
        value, _ = reduce_to(value, 1)
        value = (after[c][0][:1].astype(jnp.float32) + value).astype(jnp.bfloat16)
        results.append(value.reshape(micro, rows, width))
    result = jnp.stack(results, axis=2)
    keep = jnp.where(first, result[0], result[1])
    received = swap(jnp.where(first, result[1], result[0]))
    both = jnp.where(
        first, jnp.stack([keep, received], axis=2), jnp.stack([received, keep], axis=2)
    )
    return both.reshape(1, rows, model_width)


def solution(mesh):
    placed = (
        P(None, ("groups", "expert"), None),
        P("section", None, ("groups", "expert"), None),
        P("section", None),
        P("section", None, None),
        P("section", None, "expert"),
        P("section", None, "expert"),
        P("section", "expert", None),
    )
    return jax.shard_map(
        local,
        mesh=mesh,
        in_specs=placed,
        out_specs=P("section", ("groups", "expert"), None),
        check_vma=False,
    )
```

```python
import functools

import jax
import jax.numpy as jnp
from jax import lax
from jax.experimental import pallas as pl
from jax.experimental.pallas import tpu as pltpu
from jax.sharding import PartitionSpec as P

FF = 1024
EXPERTS = 16
EPSILON = 1e-06
CHUNKS = 2
COPIES = 8
LANES = 128
VMEM_BYTES = 62 << 20
IN_VMEM = pl.BlockSpec(memory_space=pltpu.VMEM)
ANYWHERE = pl.BlockSpec(memory_space=pl.ANY)


def bit_orders(count):
    bits = [1 << k for k in range(count.bit_length() - 1)]
    return bits, bits[1:] + bits[:1]


def block_of(order):
    table = [0]
    for bit in reversed(order):
        table = table + [b ^ bit for b in table]
    return table


def swap_tables(count):
    first, second = (block_of(order) for order in bit_orders(count))
    return [second.index(b) for b in first], [first.index(b) for b in second]


def exchange(value, level):
    count = lax.axis_size("expert")
    orders = bit_orders(count)
    pairs = [
        (2 * e + s, 2 * (e ^ orders[s][level]) + s) for e in range(count) for s in range(2)
    ]
    return lax.ppermute(value, ("expert", "section"), pairs)


def swap(value):
    return lax.ppermute(value, "section", [(0, 1), (1, 0)])


def add(left, right):
    return left.astype(jnp.float32) + right.astype(jnp.float32)


def spread(value, level):
    while level >= 0:
        value = jnp.concatenate([value, exchange(value, level)], axis=0)
        level -= 1
    return value


def reduce_to(value, last):
    level = 0
    while value.shape[0] > last:
        half = value.shape[0] // 2
        received = exchange(value[half:], level)
        value = add(value[:half], received)
        if half > 1:
            value = value.astype(jnp.bfloat16)
        level += 1
    return value, level


def in_order(value, token):
    return lax.optimization_barrier((value, token))[0]


class Piece:
    def __init__(self, source, axis, part, parts):
        self.source, self.axis = source, axis
        self.shape = list(source.shape[1:])
        self.shape[axis] //= parts
        self.start = part * self.shape[axis]
        self.type = pltpu.VMEM(tuple(self.shape), source.dtype)
        self.nbytes = self.shape[0] * self.shape[1] * source.dtype.itemsize

    def copies(self, source, target, sems):
        rows = self.shape[0] // COPIES
        made = []
        for c in range(COPIES):
            at = pl.ds(c * rows, rows)
            if self.axis == 0:
                part = source.at[0, pl.ds(self.start + c * rows, rows)]
            else:
                part = source.at[0, at, pl.ds(self.start, self.shape[1])]
            made.append(pltpu.make_async_copy(part, target.at[at], sems.at[c]))
        return made


def call(body, layer, inputs, outputs, scratch, pieces, held, name, after=None, token=False):
    n_in, n_out, n_piece = len(inputs), len(outputs), len(pieces)
    extra = [] if after is None else [after]

    def kernel(*refs):
        refs = list(refs)
        ins, refs = refs[:n_in], refs[n_in:]
        sources, refs = refs[:n_piece], refs[n_piece + len(extra) :]
        outs, refs = refs[:n_out], refs[n_out:]
        targets, refs = refs[:n_piece], refs[n_piece:]
        if token:
            marker, refs = refs[0], refs[1:]
            marker[...] = jnp.zeros_like(marker)
        sems, refs = refs[:n_piece], refs[n_piece:]

        @pl.when(lax.axis_index("section") == layer)
        def _():
            made = []
            for piece, source, target, sem in zip(pieces, sources, targets, sems):
                made += piece.copies(source, target, sem)
            for copy in made:
                copy.start()
            if body is not None:
                body(ins, outs, refs)
            for copy in made:
                copy.wait()

    arrived = sum(piece.nbytes for piece in pieces)
    shapes = list(outputs) + [piece.type for piece in pieces]
    if token:
        shapes.append(jax.ShapeDtypeStruct((8, LANES), jnp.float32))
    results = pl.pallas_call(
        kernel,
        in_specs=[IN_VMEM] * n_in + [ANYWHERE] * (n_piece + len(extra)),
        out_specs=[IN_VMEM] * len(shapes),
        out_shape=shapes,
        scratch_shapes=[pltpu.SemaphoreType.DMA((COPIES,)) for _ in pieces] + list(scratch),
        compiler_params=pltpu.CompilerParams(
            vmem_limit_bytes=VMEM_BYTES - held - arrived, has_side_effects=False
        ),
        cost_estimate=pl.CostEstimate(
            flops=0, transcendentals=0, bytes_accessed=arrived + held // 2
        ),
        name=name,
    )(*inputs, *[piece.source for piece in pieces], *extra)
    return list(results)


def prepare(tokens, routes, width):
    micro, rows, _ = tokens.shape
    top = routes.shape[2]
    block = micro * rows

    def kernel(tokens_ref, routes_ref, out):
        section = lax.axis_index("section")
        for c in range(CHUNKS):
            at = pl.multiple_of((2 * c + section) * width, LANES)
            both = [tokens_ref[m, :, pl.ds(at, width)].astype(jnp.float32) for m in range(micro)]
            out[0, :, c * width : (c + 1) * width] = jnp.concatenate(both, 0).astype(jnp.bfloat16)
        lane = lax.broadcasted_iota(jnp.int32, (rows, LANES), 1)
        eye = lax.broadcasted_iota(jnp.int32, (rows, rows), 0) == lax.broadcasted_iota(
            jnp.int32, (rows, rows), 1
        )
        named = []
        for m in range(micro):
            value = jnp.zeros((rows, LANES), jnp.float32)
            for k in range(top):
                line = jnp.broadcast_to(routes_ref[0, m, k : k + 1].astype(jnp.float32), (rows, rows))
                column = jnp.sum(jnp.where(eye, line, 0.0), axis=1, keepdims=True)
                value = jnp.where(lane == k, column, value)
            named.append(value)
        out[0, :, CHUNKS * width :] = jnp.concatenate(named, 0).astype(jnp.bfloat16)

    return pl.pallas_call(
        kernel,
        in_specs=[IN_VMEM] * 2,
        out_specs=IN_VMEM,
        out_shape=jax.ShapeDtypeStruct((1, block, CHUNKS * width + LANES), jnp.bfloat16),
        name="prepare",
    )(tokens, routes)


def gate_up_body(chunk, width, offset, top, ins, outs, scratch):
    first, last = chunk == 0, chunk == CHUNKS - 1
    own, other, gain, router, gate_w, up_w = ins[:6]
    scaled, stats = scratch
    count, rows, _ = own.shape
    model_width = gain.shape[1]
    units = gate_w.shape[1]
    section = lax.axis_index("section")
    mine_at = pl.multiple_of(section * width, LANES)
    theirs_at = pl.multiple_of((1 - section) * width, LANES)
    base = 2 * chunk * width
    mine_gain = gain[:, pl.ds(pl.multiple_of(base + mine_at, LANES), width)]
    theirs_gain = gain[:, pl.ds(pl.multiple_of(base + theirs_at, LANES), width)]
    tables = swap_tables(count)
    lane = lax.broadcasted_iota(jnp.int32, (rows, LANES), 1)
    for p in range(count):
        at = pl.ds(p * rows, rows)
        mine = own[p, :, offset : offset + width].astype(jnp.float32)
        their_block = jnp.where(section == 0, tables[0][p], tables[1][p])
        theirs = other[their_block, :, offset : offset + width].astype(jnp.float32)
        scaled[at, pl.ds(mine_at, width)] = (mine * mine_gain).astype(jnp.bfloat16)
        scaled[at, pl.ds(theirs_at, width)] = (theirs * theirs_gain).astype(jnp.bfloat16)
        square = jnp.sum(mine * mine + theirs * theirs, axis=-1, keepdims=True)
        stats[at, :] = jnp.where(lane == EXPERTS, square, 0.0)
    logits = lax.dot_general(
        scaled[...],
        router[0, :, base : base + 2 * width],
        (((1,), (1,)), ((), ())),
        preferred_element_type=jnp.float32,
    )
    stats[:, :EXPERTS] = logits
    if not first:
        gate_in, up_in, stats_in = ins[6:9]
        stats[...] += stats_in[...]
    if last:
        named = ins[-1]
        values = stats[...]
        lanes = lax.broadcasted_iota(jnp.int32, values.shape, 1)
        total = jnp.sum(jnp.where(lanes == EXPERTS, values, 0.0), axis=-1, keepdims=True)
        factor = lax.rsqrt(total / model_width + EPSILON)
        affinity = jax.nn.sigmoid(values * factor)
        experts = named[...].astype(jnp.float32).reshape(values.shape)
        hit = jnp.zeros(values.shape, jnp.bool_)
        for k in range(top):
            hit = hit | (experts[:, k : k + 1] == lanes.astype(jnp.float32))
        picked = jnp.where(hit & (lanes < EXPERTS), affinity, 0.0)
        gates = picked / jnp.sum(picked, axis=-1, keepdims=True)
        unit_at = lax.axis_index("expert") * units
    else:
        outs[2][...] = stats[...]
    tile = min(256, units)
    for t in range(units // tile):
        at = slice(t * tile, (t + 1) * tile)
        gate_part = jnp.dot(scaled[...], gate_w[:, at], preferred_element_type=jnp.float32)
        up_part = jnp.dot(scaled[...], up_w[:, at], preferred_element_type=jnp.float32)
        if not first:
            gate_part += gate_in[:, at]
            up_part += up_in[:, at]
        if last:
            expert = (unit_at + t * tile) // FF
            weight = jnp.sum(jnp.where(lanes == expert, gates, 0.0), axis=-1, keepdims=True)
            gated = jax.nn.silu(gate_part * factor) * (up_part * (factor * weight))
            outs[0][:, at] = gated.astype(jnp.bfloat16)
        else:
            outs[0][:, at] = gate_part
            outs[1][:, at] = up_part


def gate_up(layer, chunk, own, other, offset, gain, router, weights, carried, named, top, pieces, held):
    count, rows, _ = own.shape
    total = count * rows
    units = weights[0].shape[1]
    width = weights[0].shape[0] // 2
    inputs = [own, other, gain, router, *weights, *carried]
    if chunk == CHUNKS - 1:
        inputs.append(named)
        outputs = [jax.ShapeDtypeStruct((total, units), jnp.bfloat16)]
    else:
        outputs = [
            jax.ShapeDtypeStruct((total, units), jnp.float32),
            jax.ShapeDtypeStruct((total, units), jnp.float32),
            jax.ShapeDtypeStruct((total, LANES), jnp.float32),
        ]
    scratch = [
        pltpu.VMEM((total, 2 * width), jnp.bfloat16),
        pltpu.VMEM((total, LANES), jnp.float32),
    ]
    body = functools.partial(gate_up_body, chunk, width, offset, top)
    results = call(body, layer, inputs, outputs, scratch, pieces, held, "gate_up")
    return results[: len(outputs)], results[len(outputs) :]


def down_body(ins, outs, scratch):
    hidden, weight = ins
    other_out, own_out = outs
    count, rows, width = own_out.shape
    section = lax.axis_index("section")
    tables = swap_tables(count)
    tile = 256 if width % 256 == 0 else LANES
    for out, side in ((other_out, 1 - section), (own_out, section)):
        for t in range(width // tile):
            at = pl.multiple_of(side * width + t * tile, LANES)
            part = jnp.dot(
                hidden[...], weight[:, pl.ds(at, tile)], preferred_element_type=jnp.float32
            ).astype(jnp.bfloat16)
            for p in range(count):
                block = p
                if out is other_out:
                    block = jnp.where(section == 0, tables[0][p], tables[1][p])
                out[block, :, t * tile : (t + 1) * tile] = part[p * rows : (p + 1) * rows]


def down(layer, hidden, weight, count, pieces, held):
    total, units = hidden.shape
    shape = jax.ShapeDtypeStruct((count, total // count, weight.shape[1] // 2), jnp.bfloat16)
    results = call(down_body, layer, [hidden, weight], [shape, shape], [], pieces, held, "down")
    return results[:2], results[2:]


def fetch(layer, pieces, after, held):
    results = call(None, layer, [], [], [], pieces, held, "fetch", after=after, token=True)
    return results[:-1], results[-1]


def local(tokens, routes, norm_gain, router_weight, gate_weight, up_weight, down_weight):
    count = lax.axis_size("expert")
    micro, rows, model_width = tokens.shape
    width = model_width // (2 * CHUNKS)
    top = routes.shape[-1]
    section = lax.axis_index("section")
    first = section == 0
    deepest = count.bit_length() - 2
    router = jnp.swapaxes(router_weight, 1, 2)
    gates = [Piece(gate_weight, 0, c, CHUNKS) for c in range(CHUNKS)]
    ups = [Piece(up_weight, 0, c, CHUNKS) for c in range(CHUNKS)]
    downs = [Piece(down_weight, 1, c, CHUNKS) for c in range(CHUNKS)]
    size = gates[0].nbytes

    value = prepare(tokens, jnp.swapaxes(routes, 2, 3), width)
    plan = [[gates[0]], [ups[0]], [gates[1]]]
    early = []
    for step in range(deepest + 1):
        received = exchange(value, deepest - step)
        if plan:
            todo = [p for group in plan for p in group] if step == deepest else plan[0]
            plan = [] if step == deepest else plan[1:]
            arrived, token = fetch(0, todo, value, len(early) * size)
            early += arrived
            received = in_order(received, token)
        value = jnp.concatenate([value, received], axis=0)
    gathered = (value, swap(value))
    named = value[:, :, CHUNKS * width :]

    def partials(layer, pieces, early, after_down):
        gate0, up0, gate1 = early
        own, other, offset = pieces[0]
        carried, (up1,) = gate_up(
            layer, 0, own, other, offset, norm_gain, router, [gate0, up0], [], None, top, [ups[1]], 3 * size
        )
        own, other, offset = pieces[1]
        (hidden,), (down0,) = gate_up(
            layer, 1, own, other, offset, norm_gain, router, [gate1, up1], carried, named, top, [downs[0]], 2 * size
        )
        (other0, own0), (down1,) = down(layer, hidden, down0, count, [downs[1]], size)
        (other1, own1), _ = down(layer, hidden, down1, count, [], size)
        return (own0, other0), (own1, other1)

    def join(layer, own, other):
        return jnp.where(section == layer, own, other)

    sums = partials(0, [(*gathered, c * width) for c in range(CHUNKS)], early, None)
    early = []
    moved = []
    plan = [[gates[0], ups[0]], [gates[1]]]
    for c in range(CHUNKS):
        own, other = sums[c]
        other = swap(other)
        arrived, token = fetch(1, plan[c], own, len(early) * size + size)
        early += arrived
        moved.append(in_order(join(0, own, other), token))
    after = []
    for c in range(CHUNKS):
        value, level = reduce_to(moved[c], 2)
        value = value.astype(jnp.bfloat16)
        received = exchange(value, level)
        value = add(value, jnp.flip(received, axis=0))
        mine = gathered[0][:2, :, c * width : (c + 1) * width]
        value = (mine.astype(jnp.float32) + value).astype(jnp.bfloat16)
        value = spread(value, level - 1)
        after.append((value, swap(value), 0))

    sums = partials(1, after, early, None)
    results = []
    for c in range(CHUNKS):
        own, other = sums[c]
        value, _ = reduce_to(join(1, own, swap(other)), 1)
        value = (after[c][0][:1].astype(jnp.float32) + value).astype(jnp.bfloat16)
        results.append(value.reshape(micro, rows, width))
    result = jnp.stack(results, axis=2)
    keep = jnp.where(first, result[0], result[1])
    received = swap(jnp.where(first, result[1], result[0]))
    both = jnp.where(
        first, jnp.stack([keep, received], axis=2), jnp.stack([received, keep], axis=2)
    )
    return both.reshape(1, rows, model_width)


def solution(mesh):
    placed = (
        P(None, ("groups", "expert"), None),
        P("section", None, ("groups", "expert"), None),
        P("section", None),
        P("section", None, None),
        P("section", None, "expert"),
        P("section", None, "expert"),
        P("section", "expert", None),
    )
    return jax.shard_map(
        local,
        mesh=mesh,
        in_specs=placed,
        out_specs=P("section", ("groups", "expert"), None),
        check_vma=False,
    )
```

```python
import functools

import jax
import jax.numpy as jnp
from jax import lax
from jax.experimental import pallas as pl
from jax.experimental.pallas import tpu as pltpu
from jax.sharding import PartitionSpec as P

FF = 1024
EXPERTS = 16
EPSILON = 1e-06
CHUNKS = 2
LANES = 128
MIB = 1 << 20
IN_VMEM = pl.BlockSpec(memory_space=pltpu.VMEM)
ANYWHERE = pl.BlockSpec(memory_space=pl.ANY)


def bit_orders(count):
    bits = [1 << k for k in range(count.bit_length() - 1)]
    return bits, bits[1:2] + bits[:1] + bits[2:]


def block_of(order):
    table = [0]
    for bit in reversed(order):
        table = table + [b ^ bit for b in table]
    return table


def swap_tables(count):
    first, second = (block_of(order) for order in bit_orders(count))
    return [second.index(b) for b in first], [first.index(b) for b in second]


def exchange(value, level):
    count = lax.axis_size("expert")
    orders = bit_orders(count)
    pairs = [
        (2 * e + s, 2 * (e ^ orders[s][level]) + s) for e in range(count) for s in range(2)
    ]
    return lax.ppermute(value, ("expert", "section"), pairs)


def swap(value):
    return lax.ppermute(value, "section", [(0, 1), (1, 0)])


def add(left, right):
    return left.astype(jnp.float32) + right.astype(jnp.float32)


def reduce_to(value, last):
    level = 0
    while value.shape[0] > last:
        half = value.shape[0] // 2
        received = exchange(value[half:], level)
        value = add(value[:half], received)
        if half > 1:
            value = value.astype(jnp.bfloat16)
        level += 1
    return value, level


def after_token(value, token):
    return value + token[None]


class Arena:
    def __init__(self, weights, width, slots, top):
        self.weights, self.width, self.slots = weights, width, slots
        self.units = weights[0].shape[2]
        self.blocks = weights[0].shape[1] // width
        self.tile = min(256, self.units)
        self.loads = 3 * self.blocks
        self.slot_rows = width * self.units // self.tile
        self.nbytes = slots * self.slot_rows * self.tile * 2
        self.limit = top - self.nbytes
        self.type = pltpu.VMEM((slots * self.slot_rows, self.tile), weights[0].dtype)

    def at(self, load):
        return load % self.slots * self.slot_rows

    def down_load(self, block):
        return 2 * self.blocks + block

    def copies(self, load, sources, arena, sems):
        made = []
        if load < 2 * self.blocks:
            source, block, depth = sources[load % 2], load // 2, self.width
            corners = [(block * depth, t * self.tile) for t in range(self.units // self.tile)]
        else:
            source, block, depth = sources[2], load - 2 * self.blocks, self.units
            corners = [(0, block * self.width + t * self.tile) for t in range(self.width // self.tile)]
        for t, (row, column) in enumerate(corners):
            made.append(
                pltpu.make_async_copy(
                    source.at[0, pl.ds(row, depth), pl.ds(column, self.tile)],
                    arena.at[pl.ds(self.at(load) + t * depth, depth)],
                    sems.at[t],
                )
            )
        return made


def call(body, layer, place, arena, inputs, outputs, scratch, loads, name, after=None, token=None, zeros=False, specs=None):
    n_in, n_out = len(inputs), len(outputs)
    extra = [] if after is None else [after]
    held = [] if arena is None else [arena]
    most = max(place.units, place.width) // place.tile

    def kernel(*refs):
        refs = list(refs)
        ins, refs = refs[:n_in], refs[n_in:]
        sources, refs = refs[:3], refs[3 + len(extra) + len(held) :]
        outs, refs = refs[:n_out], refs[n_out:]
        memory, refs = refs[0], refs[1:]
        if token is not None:
            marker, refs = refs[0], refs[1:]
            marker[...] = jnp.zeros_like(marker)
        sems, refs = refs[0], refs[1:]
        flying = {}

        def start(load):
            flying[load] = place.copies(load, sources, memory, sems.at[loads.index(load)])
            for copy in flying[load]:
                copy.start()

        def wait(load):
            for copy in flying.pop(load, []):
                copy.wait()

        def work():
            body(ins, outs, refs, memory, start, wait)
            for load in list(flying):
                wait(load)

        if layer is None:
            work()
        else:
            here = lax.axis_index("section") == layer
            pl.when(here)(work)
            if zeros:

                @pl.when(jnp.logical_not(here))
                def _():
                    for out in outs:
                        out[...] = jnp.zeros_like(out)

    shapes = list(outputs) + [place.type]
    if token is not None:
        shapes.append(pltpu.VMEM(token, jnp.bfloat16))
    moved = max(len(loads), 1) * place.slot_rows * place.tile * 2
    results = pl.pallas_call(
        kernel,
        in_specs=(specs or [IN_VMEM] * n_in) + [ANYWHERE] * 3 + [IN_VMEM] * (len(extra) + len(held)),
        out_specs=[IN_VMEM] * len(shapes),
        out_shape=shapes,
        input_output_aliases={n_in + 3 + len(extra): n_out} if held else {},
        scratch_shapes=[pltpu.SemaphoreType.DMA((max(len(loads), 1), most))] + list(scratch),
        compiler_params=pltpu.CompilerParams(vmem_limit_bytes=place.limit),
        cost_estimate=pl.CostEstimate(flops=0, transcendentals=0, bytes_accessed=moved),
        name=name,
    )(*inputs, *place.weights, *extra, *held)
    return list(results)


def prepare(tokens, routes, width):
    micro, rows, _ = tokens.shape
    top = routes.shape[2]
    block = micro * rows

    def kernel(tokens_ref, routes_ref, *outs):
        section = lax.axis_index("section")
        for c in range(CHUNKS):
            at = pl.multiple_of((2 * c + section) * width, LANES)
            both = [tokens_ref[m, :, pl.ds(at, width)].astype(jnp.float32) for m in range(micro)]
            outs[c][0, :, :width] = jnp.concatenate(both, 0).astype(jnp.bfloat16)
        lane = lax.broadcasted_iota(jnp.int32, (rows, LANES), 1)
        eye = lax.broadcasted_iota(jnp.int32, (rows, rows), 0) == lax.broadcasted_iota(
            jnp.int32, (rows, rows), 1
        )
        named = []
        for m in range(micro):
            value = jnp.zeros((rows, LANES), jnp.float32)
            for k in range(top):
                line = jnp.broadcast_to(routes_ref[0, m, k : k + 1].astype(jnp.float32), (rows, rows))
                column = jnp.sum(jnp.where(eye, line, 0.0), axis=1, keepdims=True)
                value = jnp.where(lane == k, column, value)
            named.append(value)
        outs[0][0, :, width:] = jnp.concatenate(named, 0).astype(jnp.bfloat16)

    shapes = [
        jax.ShapeDtypeStruct((1, block, width + (LANES if c == 0 else 0)), jnp.bfloat16)
        for c in range(CHUNKS)
    ]
    return pl.pallas_call(
        kernel,
        in_specs=[IN_VMEM] * 2,
        out_specs=[IN_VMEM] * CHUNKS,
        out_shape=shapes,
        name="prepare",
    )(tokens, routes)


def layer_body(place, top, ins, outs, scratch, memory, start, wait):
    pairs = [ins[2 * c : 2 * c + 2] for c in range(CHUNKS)]
    gain, router, named = ins[2 * CHUNKS :]
    scaled, stats, gate_sum, up_sum, hidden, routes, sem = scratch
    count, rows, width = outs[0].shape
    tile, units, blocks = place.tile, place.units, place.blocks
    model_width = gain.shape[1]
    section = lax.axis_index("section")
    tables = swap_tables(count)
    lane = lax.broadcasted_iota(jnp.int32, (rows, LANES), 1)
    bring = pltpu.make_async_copy(named.at[:, :, pl.ds(width, LANES)], routes, sem)
    bring.start()

    def used(load):
        if load + place.slots < place.loads:
            start(load + place.slots)

    def block_for_other(p):
        return jnp.where(section == 0, tables[0][p], tables[1][p])

    for chunk, (own, other) in enumerate(pairs):
        mine_at = pl.multiple_of((2 * chunk + section) * width, LANES)
        theirs_at = pl.multiple_of((2 * chunk + 1 - section) * width, LANES)
        mine_gain = gain[:, pl.ds(mine_at, width)]
        theirs_gain = gain[:, pl.ds(theirs_at, width)]
        for p in range(count):
            at = pl.ds(p * rows, rows)
            mine = own[p, :, :width].astype(jnp.float32)
            theirs = other[block_for_other(p), :, :width].astype(jnp.float32)
            scaled[at, pl.ds(mine_at, width)] = (mine * mine_gain).astype(jnp.bfloat16)
            scaled[at, pl.ds(theirs_at, width)] = (theirs * theirs_gain).astype(jnp.bfloat16)
            square = jnp.sum(mine * mine + theirs * theirs, axis=-1, keepdims=True)
            square = jnp.where(lane == EXPERTS, square, 0.0)
            stats[at, :] = square if chunk == 0 else stats[at, :] + square
    stats[:, :EXPERTS] = lax.dot_general(
        scaled[...], router[0], (((1,), (1,)), ((), ())), preferred_element_type=jnp.float32
    )
    values = stats[...]
    lanes = lax.broadcasted_iota(jnp.int32, values.shape, 1)
    total = jnp.sum(jnp.where(lanes == EXPERTS, values, 0.0), axis=-1, keepdims=True)
    factor = lax.rsqrt(total / model_width + EPSILON)
    affinity = jax.nn.sigmoid(values * factor)
    bring.wait()
    experts = routes[...].astype(jnp.float32).reshape(values.shape)
    hit = jnp.zeros(values.shape, jnp.bool_)
    for k in range(top):
        hit = hit | (experts[:, k : k + 1] == lanes.astype(jnp.float32))
    picked = jnp.where(hit & (lanes < EXPERTS), affinity, 0.0)
    gates = picked / jnp.sum(picked, axis=-1, keepdims=True)
    unit_at = lax.axis_index("expert") * units

    for block in range(blocks):
        value = scaled.at[:, block * width : (block + 1) * width]
        for side, sums in enumerate((gate_sum, up_sum)):
            load = 2 * block + side
            wait(load)
            for t in range(units // tile):
                at = slice(t * tile, (t + 1) * tile)
                part = jnp.dot(
                    value[...],
                    memory[pl.ds(place.at(load) + t * width, width)],
                    preferred_element_type=jnp.float32,
                )
                if block > 0:
                    part += sums[:, at]
                if block < blocks - 1 or side == 0:
                    sums[:, at] = part
                    continue
                expert = (unit_at + t * tile) // FF
                weight = jnp.sum(jnp.where(lanes == expert, gates, 0.0), axis=-1, keepdims=True)
                gated = jax.nn.silu(gate_sum[:, at] * factor) * (part * (factor * weight))
                hidden[:, at] = gated.astype(jnp.bfloat16)
            used(load)

    for chunk in range(CHUNKS):
        places = []
        for side in range(2):
            load = place.down_load(2 * chunk + side)
            wait(load)
            places.append(place.at(load))
        for own in range(2):
            out = outs[2 * chunk + own]
            side = section if own else 1 - section
            base = jnp.where(side == 0, places[0], places[1])
            for t in range(width // tile):
                at = pl.multiple_of(base + t * units, 16)
                part = jnp.dot(
                    hidden[...], memory[pl.ds(at, units)], preferred_element_type=jnp.float32
                ).astype(jnp.bfloat16)
                to = slice(t * tile, (t + 1) * tile)
                for p in range(count):
                    out[p if own else block_for_other(p), :, to] = part[p * rows : (p + 1) * rows]
        for side in range(2):
            used(place.down_load(2 * chunk + side))


def run_layer(layer, place, arena, pairs, gain, router, named, top):
    count, rows, _ = pairs[0][0].shape
    total = count * rows
    shape = jax.ShapeDtypeStruct((count, rows, place.width), jnp.bfloat16)
    scratch = [
        pltpu.VMEM((total, gain.shape[1]), jnp.bfloat16),
        pltpu.VMEM((total, LANES), jnp.float32),
        pltpu.VMEM((total, place.units), jnp.float32),
        pltpu.VMEM((total, place.units), jnp.float32),
        pltpu.VMEM((total, place.units), jnp.bfloat16),
        pltpu.VMEM((count, rows, LANES), jnp.bfloat16),
        pltpu.SemaphoreType.DMA,
    ]
    inputs = [value for pair in pairs for value in pair] + [gain, router, named]
    specs = [IN_VMEM] * (len(inputs) - 1) + [ANYWHERE]
    results = call(
        functools.partial(layer_body, place, top),
        layer, place, arena, inputs, [shape] * (2 * CHUNKS), scratch,
        list(range(place.slots, place.loads)), "layer", zeros=True, specs=specs,
    )
    return results[:-1], results[-1]


def run_layer_plainly(layer, weights, pairs, gain, router, named, top):
    count, rows, _ = pairs[0][0].shape
    model_width = gain.shape[1]
    width = model_width // (2 * CHUNKS)
    units = weights[0].shape[2]
    first = lax.axis_index("section") == 0
    tables = jnp.array(swap_tables(count), jnp.int32)
    table = jnp.where(first, tables[0], tables[1])
    back = jnp.where(first, tables[1], tables[0])
    columns = []
    for own, other in pairs:
        own, other = own[:, :, :width], other[:, :, :width][table]
        columns += [jnp.where(first, own, other), jnp.where(first, other, own)]
    values = jnp.concatenate(columns, axis=-1).reshape(count * rows, model_width).astype(jnp.float32)
    factor = lax.rsqrt(jnp.mean(values * values, axis=-1, keepdims=True) + EPSILON)
    scaled = (values * gain).astype(jnp.bfloat16)

    def product(left, right):
        return jnp.dot(left, right, preferred_element_type=jnp.float32)

    affinity = jax.nn.sigmoid(product(scaled, router[0].T) * factor)
    experts = named[:, :, width : width + top].reshape(count * rows, top).astype(jnp.int32)
    hit = jnp.any(experts[:, :, None] == jnp.arange(EXPERTS, dtype=jnp.int32), axis=1)
    picked = jnp.where(hit, affinity, 0.0)
    gates = picked / jnp.sum(picked, axis=-1, keepdims=True)
    of_unit = (lax.axis_index("expert") * units + jnp.arange(units, dtype=jnp.int32)) // FF
    weight = jnp.take(gates, of_unit, axis=1)
    up_part = product(scaled, weights[1][0]) * (factor * weight)
    hidden = (jax.nn.silu(product(scaled, weights[0][0]) * factor) * up_part).astype(jnp.bfloat16)
    out = product(hidden, weights[2][0]).astype(jnp.bfloat16)
    out = out.reshape(count, rows, CHUNKS, 2, width)
    out = jnp.where(lax.axis_index("section") == layer, out, jnp.zeros_like(out))
    parts = []
    for c in range(CHUNKS):
        left, right = out[:, :, c, 0], out[:, :, c, 1]
        parts += [jnp.where(first, right, left)[back], jnp.where(first, left, right)]
    return parts


def fetch(place, arena, loads, after, token):
    def body(ins, outs, scratch, memory, start, wait):
        for load in loads:
            start(load)

    return call(body, None, place, arena, [], [], [], loads, "fetch", after=after, token=token)


def local(tokens, routes, norm_gain, router_weight, gate_weight, up_weight, down_weight):
    count = lax.axis_size("expert")
    micro, rows, model_width = tokens.shape
    width = model_width // (2 * CHUNKS)
    top = routes.shape[-1]
    section = lax.axis_index("section")
    first = section == 0
    deepest = count.bit_length() - 2
    router = jnp.swapaxes(router_weight, 1, 2)
    weights = (gate_weight, up_weight, down_weight)
    held = count * micro * rows <= 2 * LANES
    place = Arena(weights, width, 6, 62 * MIB)

    def partials(layer, pairs):
        nonlocal arena
        if held:
            parts, arena = run_layer(layer, place, arena, pairs, norm_gain, router, named, top)
        else:
            parts = run_layer_plainly(layer, weights, pairs, norm_gain, router, named, top)
        moved = [swap(parts[2 * c]) for c in range(CHUNKS)]
        return [add(parts[2 * c + 1], moved[c]).astype(jnp.bfloat16) for c in range(CHUNKS)]

    gathered = list(prepare(tokens, jnp.swapaxes(routes, 2, 3), width))
    arena = None
    loads = list(range(place.slots))
    for level in reversed(range(deepest + 1)):
        received = [exchange(value, level) for value in gathered]
        if held:
            todo, loads = (loads[:2], loads[2:]) if level > 0 else (loads, [])
            arena, token = fetch(place, arena, todo, gathered[0], received[0].shape[1:])
            received[0] = after_token(received[0], token)
        gathered = [jnp.concatenate(pair, axis=0) for pair in zip(gathered, received)]
    named = gathered[0]
    moved = partials(0, [(value, swap(value)) for value in gathered])

    after = list(moved)
    for level in range(deepest):
        for c in range(CHUNKS):
            half = after[c].shape[0] // 2
            received = exchange(after[c][half:], level)
            after[c] = add(after[c][:half], received).astype(jnp.bfloat16)
    for c in range(CHUNKS):
        value = add(after[c], jnp.flip(exchange(after[c], deepest), axis=0))
        residual = gathered[c][:2, :, :width].astype(jnp.float32)
        after[c] = (residual + value).astype(jnp.bfloat16)
    own_after = [value[:1] for value in after]
    for level in reversed(range(deepest)):
        for c in range(CHUNKS):
            after[c] = jnp.concatenate([after[c], exchange(after[c], level)], axis=0)
    sums = partials(1, [(value, swap(value)) for value in after])
    results = []
    for c in range(CHUNKS):
        value, _ = reduce_to(sums[c], 1)
        value = (own_after[c].astype(jnp.float32) + value).astype(jnp.bfloat16)
        results.append(value.reshape(micro, rows, width))
    result = jnp.stack(results, axis=2)
    keep = jnp.where(first, result[0], result[1])
    received = swap(jnp.where(first, result[1], result[0]))
    both = jnp.where(
        first, jnp.stack([keep, received], axis=2), jnp.stack([received, keep], axis=2)
    )
    return both.reshape(1, rows, model_width)


def solution(mesh):
    placed = (
        P(None, ("groups", "expert"), None),
        P("section", None, ("groups", "expert"), None),
        P("section", None),
        P("section", None, None),
        P("section", None, "expert"),
        P("section", None, "expert"),
        P("section", "expert", None),
    )
    return jax.shard_map(
        local,
        mesh=mesh,
        in_specs=placed,
        out_specs=P("section", ("groups", "expert"), None),
        check_vma=False,
    )
```

```python
import functools

import jax
import jax.numpy as jnp
from jax import lax
from jax.experimental import pallas as pl
from jax.experimental.pallas import tpu as pltpu
from jax.sharding import PartitionSpec as P

FF = 1024
EXPERTS = 16
EPSILON = 1e-06
CHUNKS = 2
LANES = 128
SLOTS = 6
RESIDENT = 6
FETCHES = (2, 2, 2)
TOP = 60 << 20
IN_VMEM = pl.BlockSpec(memory_space=pltpu.VMEM)
ANYWHERE = pl.BlockSpec(memory_space=pl.ANY)


def bit_orders(count):
    bits = [1 << k for k in range(count.bit_length() - 1)]
    return bits, bits[1:2] + bits[:1] + bits[2:]


def block_of(order):
    table = [0]
    for bit in reversed(order):
        table = table + [b ^ bit for b in table]
    return table


def swap_tables(count):
    first, second = (block_of(order) for order in bit_orders(count))
    return [second.index(b) for b in first], [first.index(b) for b in second]


def exchange(value, level):
    count = lax.axis_size("expert")
    orders = bit_orders(count)
    pairs = [
        (2 * e + s, 2 * (e ^ orders[s][level]) + s) for e in range(count) for s in range(2)
    ]
    return lax.ppermute(value, ("expert", "section"), pairs)


def swap(value):
    return lax.ppermute(value, "section", [(0, 1), (1, 0)])


def add(left, right):
    return left.astype(jnp.float32) + right.astype(jnp.float32)


def next_step(value, level):
    half = value.shape[0] // 2
    received = exchange(value[half:], level)
    return add(value[:half], received).astype(jnp.bfloat16)


def cross(value, flip, to_other):
    count = lax.axis_size("expert")
    bit = bit_orders(count)[0][-1] if flip else 0
    pairs = [(2 * e + s, 2 * (e ^ bit) + (s ^ to_other)) for e in range(count) for s in range(2)]
    return lax.ppermute(value, ("expert", "section"), pairs)


def after_token(value, token):
    return value + token[None]


class Arena:
    def __init__(self, weights, width, slots, resident, top):
        self.resident = resident
        self.weights, self.width, self.slots = weights, width, slots
        self.units = weights[0].shape[2]
        self.blocks = weights[0].shape[1] // width
        self.tile = min(256, self.units)
        self.loads = 3 * self.blocks
        self.slot_rows = width * self.units // self.tile
        self.nbytes = slots * self.slot_rows * self.tile * 2
        self.limit = top - self.nbytes
        self.type = pltpu.VMEM((slots * self.slot_rows, self.tile), weights[0].dtype)

    def at(self, load):
        return load % self.slots * self.slot_rows

    def down_load(self, block):
        return 2 * self.blocks + block

    def copies(self, load, sources, arena, sems):
        made = []
        if load < 2 * self.blocks:
            source, block, depth = sources[load % 2], load // 2, self.width
            corners = [(block * depth, t * self.tile) for t in range(self.units // self.tile)]
        else:
            source, block, depth = sources[2], load - 2 * self.blocks, self.units
            corners = [(0, block * self.width + t * self.tile) for t in range(self.width // self.tile)]
        for t, (row, column) in enumerate(corners):
            made.append(
                pltpu.make_async_copy(
                    source.at[0, pl.ds(row, depth), pl.ds(column, self.tile)],
                    arena.at[pl.ds(self.at(load) + t * depth, depth)],
                    sems.at[t],
                )
            )
        return made


def call(body, layer, place, arena, inputs, outputs, scratch, loads, name, after=None, token=None, zeros=False, specs=None):
    n_in, n_out = len(inputs), len(outputs)
    extra = [] if after is None else [after]
    held = [] if arena is None else [arena]
    most = max(place.units, place.width) // place.tile

    def kernel(*refs):
        refs = list(refs)
        ins, refs = refs[:n_in], refs[n_in:]
        sources, refs = refs[:3], refs[3 + len(extra) + len(held) :]
        outs, refs = refs[:n_out], refs[n_out:]
        memory, refs = refs[0], refs[1:]
        if token is not None:
            marker, refs = refs[0], refs[1:]
            marker[...] = jnp.zeros_like(marker)
        sems, refs = refs[0], refs[1:]
        flying = {}

        def start(load):
            flying[load] = place.copies(load, sources, memory, sems.at[loads.index(load)])
            for copy in flying[load]:
                copy.start()

        def wait(load):
            for copy in flying.pop(load, []):
                copy.wait()

        def work():
            body(ins, outs, refs, memory, start, wait)
            for load in list(flying):
                wait(load)

        if layer is None:
            work()
        else:
            here = lax.axis_index("section") == layer
            pl.when(here)(work)
            if zeros:

                @pl.when(jnp.logical_not(here))
                def _():
                    for out in outs:
                        out[...] = jnp.zeros_like(out)

    shapes = list(outputs) + [place.type]
    if token is not None:
        shapes.append(pltpu.VMEM(token, jnp.bfloat16))
    moved = max(len(loads), 1) * place.slot_rows * place.tile * 2
    results = pl.pallas_call(
        kernel,
        in_specs=(specs or [IN_VMEM] * n_in) + [ANYWHERE] * (3 + len(extra)) + [IN_VMEM] * len(held),
        out_specs=[IN_VMEM] * len(shapes),
        out_shape=shapes,
        input_output_aliases={n_in + 3 + len(extra): n_out} if held else {},
        scratch_shapes=[pltpu.SemaphoreType.DMA((max(len(loads), 1), most))] + list(scratch),
        compiler_params=pltpu.CompilerParams(vmem_limit_bytes=place.limit),
        cost_estimate=pl.CostEstimate(flops=0, transcendentals=0, bytes_accessed=moved),
        name=name,
    )(*inputs, *place.weights, *extra, *held)
    return list(results)


def prepare(tokens, routes, width):
    micro, rows, _ = tokens.shape
    top = routes.shape[2]
    block = micro * rows

    def kernel(tokens_ref, routes_ref, out):
        section = lax.axis_index("section")
        for c in range(CHUNKS):
            at = pl.multiple_of((2 * c + section) * width, LANES)
            both = [tokens_ref[m, :, pl.ds(at, width)].astype(jnp.float32) for m in range(micro)]
            out[0, :, c * width : (c + 1) * width] = jnp.concatenate(both, 0).astype(jnp.bfloat16)
        lane = lax.broadcasted_iota(jnp.int32, (rows, LANES), 1)
        eye = lax.broadcasted_iota(jnp.int32, (rows, rows), 0) == lax.broadcasted_iota(
            jnp.int32, (rows, rows), 1
        )
        named = []
        for m in range(micro):
            value = jnp.zeros((rows, LANES), jnp.float32)
            for k in range(top):
                line = jnp.broadcast_to(routes_ref[0, m, k : k + 1].astype(jnp.float32), (rows, rows))
                column = jnp.sum(jnp.where(eye, line, 0.0), axis=1, keepdims=True)
                value = jnp.where(lane == k, column, value)
            named.append(value)
        out[0, :, CHUNKS * width :] = jnp.concatenate(named, 0).astype(jnp.bfloat16)

    return pl.pallas_call(
        kernel,
        in_specs=[IN_VMEM] * 2,
        out_specs=IN_VMEM,
        out_shape=jax.ShapeDtypeStruct((1, block, CHUNKS * width + LANES), jnp.bfloat16),
        name="prepare",
    )(tokens, routes)


def layer_body(place, top, together, ins, outs, scratch, memory, start, wait):
    gain, router, named = ins[-3:]
    scaled, stats, gate_sum, up_sum, hidden, routes, sem = scratch
    count, rows, width = outs[0].shape
    tile, units, blocks = place.tile, place.units, place.blocks
    model_width = gain.shape[1]
    section = lax.axis_index("section")
    tables = swap_tables(count)
    lane = lax.broadcasted_iota(jnp.int32, (rows, LANES), 1)
    bring = pltpu.make_async_copy(named.at[:, :, pl.ds(CHUNKS * width, LANES)], routes, sem)
    bring.start()
    for load in range(place.resident, place.slots):
        start(load)

    def used(load):
        if load + place.slots < place.loads:
            start(load + place.slots)

    def block_for_other(p):
        return jnp.where(section == 0, tables[0][p], tables[1][p])

    for chunk in range(CHUNKS):
        own, other = ins[:2] if together else ins[2 * chunk : 2 * chunk + 2]
        columns = slice(chunk * width, (chunk + 1) * width) if together else slice(0, width)
        mine_at = pl.multiple_of((2 * chunk + section) * width, LANES)
        theirs_at = pl.multiple_of((2 * chunk + 1 - section) * width, LANES)
        mine_gain = gain[:, pl.ds(mine_at, width)]
        theirs_gain = gain[:, pl.ds(theirs_at, width)]
        for p in range(count):
            at = pl.ds(p * rows, rows)
            mine = own[p, :, columns].astype(jnp.float32)
            theirs = other[block_for_other(p), :, columns].astype(jnp.float32)
            scaled[at, pl.ds(mine_at, width)] = (mine * mine_gain).astype(jnp.bfloat16)
            scaled[at, pl.ds(theirs_at, width)] = (theirs * theirs_gain).astype(jnp.bfloat16)
            square = jnp.sum(mine * mine + theirs * theirs, axis=-1, keepdims=True)
            square = jnp.where(lane == EXPERTS, square, 0.0)
            stats[at, :] = square if chunk == 0 else stats[at, :] + square
    stats[:, :EXPERTS] = lax.dot_general(
        scaled[...], router[0], (((1,), (1,)), ((), ())), preferred_element_type=jnp.float32
    )
    values = stats[...]
    lanes = lax.broadcasted_iota(jnp.int32, values.shape, 1)
    total = jnp.sum(jnp.where(lanes == EXPERTS, values, 0.0), axis=-1, keepdims=True)
    factor = lax.rsqrt(total / model_width + EPSILON)
    affinity = jax.nn.sigmoid(values * factor)
    bring.wait()
    experts = routes[...].astype(jnp.float32).reshape(values.shape)
    hit = jnp.zeros(values.shape, jnp.bool_)
    for k in range(top):
        hit = hit | (experts[:, k : k + 1] == lanes.astype(jnp.float32))
    picked = jnp.where(hit & (lanes < EXPERTS), affinity, 0.0)
    gates = picked / jnp.sum(picked, axis=-1, keepdims=True)
    unit_at = lax.axis_index("expert") * units

    for block in range(blocks):
        value = scaled.at[:, block * width : (block + 1) * width]
        for side, sums in enumerate((gate_sum, up_sum)):
            load = 2 * block + side
            wait(load)
            for t in range(units // tile):
                at = slice(t * tile, (t + 1) * tile)
                part = jnp.dot(
                    value[...],
                    memory[pl.ds(place.at(load) + t * width, width)],
                    preferred_element_type=jnp.float32,
                )
                if block > 0:
                    part += sums[:, at]
                if block < blocks - 1 or side == 0:
                    sums[:, at] = part
                    continue
                expert = (unit_at + t * tile) // FF
                weight = jnp.sum(jnp.where(lanes == expert, gates, 0.0), axis=-1, keepdims=True)
                gated = jax.nn.silu(gate_sum[:, at] * factor) * (part * (factor * weight))
                hidden[:, at] = gated.astype(jnp.bfloat16)
            used(load)

    for chunk in range(CHUNKS):
        places = []
        for side in range(2):
            load = place.down_load(2 * chunk + side)
            wait(load)
            places.append(place.at(load))
        for own in range(2):
            out = outs[2 * chunk + own]
            side = section if own else 1 - section
            base = jnp.where(side == 0, places[0], places[1])
            for t in range(width // tile):
                at = pl.multiple_of(base + t * units, 16)
                part = jnp.dot(
                    hidden[...], memory[pl.ds(at, units)], preferred_element_type=jnp.float32
                ).astype(jnp.bfloat16)
                to = slice(t * tile, (t + 1) * tile)
                for p in range(count):
                    out[p if own else block_for_other(p), :, to] = part[p * rows : (p + 1) * rows]
        for side in range(2):
            used(place.down_load(2 * chunk + side))


def run_layer(layer, place, arena, pairs, gain, router, named, top):
    count, rows, _ = pairs[0][0].shape
    total = count * rows
    shape = pltpu.VMEM((count, rows, place.width), jnp.bfloat16)
    scratch = [
        pltpu.VMEM((total, gain.shape[1]), jnp.bfloat16),
        pltpu.VMEM((total, LANES), jnp.float32),
        pltpu.VMEM((total, place.units), jnp.float32),
        pltpu.VMEM((total, place.units), jnp.float32),
        pltpu.VMEM((total, place.units), jnp.bfloat16),
        pltpu.VMEM((count, rows, LANES), jnp.bfloat16),
        pltpu.SemaphoreType.DMA,
    ]
    inputs = [value for pair in pairs for value in pair] + [gain, router, named]
    specs = [IN_VMEM] * (len(inputs) - 1) + [ANYWHERE]
    results = call(
        functools.partial(layer_body, place, top, len(pairs) == 1),
        layer, place, arena, inputs, [shape] * (2 * CHUNKS), scratch,
        list(range(place.resident, place.loads)), "layer", zeros=True, specs=specs,
    )
    return results[:-1], results[-1]


def run_layer_plainly(layer, weights, pairs, gain, router, named, top):
    count, rows, _ = pairs[0][0].shape
    model_width = gain.shape[1]
    width = model_width // (2 * CHUNKS)
    units = weights[0].shape[2]
    first = lax.axis_index("section") == 0
    tables = jnp.array(swap_tables(count), jnp.int32)
    table = jnp.where(first, tables[0], tables[1])
    back = jnp.where(first, tables[1], tables[0])
    columns = []
    if len(pairs) == 1:
        pairs = [
            [side[:, :, c * width : (c + 1) * width] for side in pairs[0]] for c in range(CHUNKS)
        ]
    for own, other in pairs:
        other = other[table]
        columns += [jnp.where(first, own, other), jnp.where(first, other, own)]
    values = jnp.concatenate(columns, axis=-1).reshape(count * rows, model_width).astype(jnp.float32)
    factor = lax.rsqrt(jnp.mean(values * values, axis=-1, keepdims=True) + EPSILON)
    scaled = (values * gain).astype(jnp.bfloat16)

    def product(left, right):
        return jnp.dot(left, right, preferred_element_type=jnp.float32)

    affinity = jax.nn.sigmoid(product(scaled, router[0].T) * factor)
    experts = named[:, :, CHUNKS * width : CHUNKS * width + top].reshape(count * rows, top).astype(jnp.int32)
    hit = jnp.any(experts[:, :, None] == jnp.arange(EXPERTS, dtype=jnp.int32), axis=1)
    picked = jnp.where(hit, affinity, 0.0)
    gates = picked / jnp.sum(picked, axis=-1, keepdims=True)
    of_unit = (lax.axis_index("expert") * units + jnp.arange(units, dtype=jnp.int32)) // FF
    weight = jnp.take(gates, of_unit, axis=1)
    up_part = product(scaled, weights[1][0]) * (factor * weight)
    hidden = (jax.nn.silu(product(scaled, weights[0][0]) * factor) * up_part).astype(jnp.bfloat16)
    out = product(hidden, weights[2][0]).astype(jnp.bfloat16)
    out = out.reshape(count, rows, CHUNKS, 2, width)
    out = jnp.where(lax.axis_index("section") == layer, out, jnp.zeros_like(out))
    parts = []
    for c in range(CHUNKS):
        left, right = out[:, :, c, 0], out[:, :, c, 1]
        parts += [jnp.where(first, right, left)[back], jnp.where(first, left, right)]
    return parts


def fetch(place, arena, loads, after, token):
    def body(ins, outs, scratch, memory, start, wait):
        for load in loads:
            start(load)

    return call(body, None, place, arena, [], [], [], loads, "fetch", after=after, token=token)


def local(tokens, routes, norm_gain, router_weight, gate_weight, up_weight, down_weight):
    count = lax.axis_size("expert")
    micro, rows, model_width = tokens.shape
    width = model_width // (2 * CHUNKS)
    top = routes.shape[-1]
    section = lax.axis_index("section")
    first = section == 0
    deepest = count.bit_length() - 2
    router = jnp.swapaxes(router_weight, 1, 2)
    weights = (gate_weight, up_weight, down_weight)
    held = count * micro * rows <= 2 * LANES
    place = Arena(weights, width, SLOTS, RESIDENT, TOP)

    def partials(layer, pairs):
        nonlocal arena
        if held:
            parts, arena = run_layer(layer, place, arena, pairs, norm_gain, router, named, top)
        else:
            parts = run_layer_plainly(layer, weights, pairs, norm_gain, router, named, top)
        moved = [swap(parts[2 * c]) for c in range(CHUNKS)]
        return [add(parts[2 * c + 1], moved[c]).astype(jnp.bfloat16) for c in range(CHUNKS)]

    gathered = prepare(tokens, jnp.swapaxes(routes, 2, 3), width)
    arena = None
    loads = list(range(RESIDENT))
    fetches = FETCHES
    for level in reversed(range(deepest + 1)):
        received = exchange(gathered, level)
        if held and fetches:
            todo, loads, fetches = loads[: fetches[0]], loads[fetches[0] :], fetches[1:]
            arena, token = fetch(place, arena, todo, gathered, received.shape[1:])
            received = after_token(received, token)
        gathered = jnp.concatenate([gathered, received], axis=0)
    if held and loads:
        arena, _ = fetch(place, arena, loads, gathered, (8, LANES))
    named = gathered
    moved = partials(0, [(gathered, swap(gathered))])

    after = list(moved)
    for level in range(deepest):
        after = [next_step(value, level) for value in after]
    for c in range(CHUNKS):
        value = add(after[c], jnp.flip(exchange(after[c], deepest), axis=0))
        residual = gathered[:2, :, c * width : (c + 1) * width].astype(jnp.float32)
        after[c] = (residual + value).astype(jnp.bfloat16)
    own_after = [value[:1] for value in after]
    for level in reversed(range(deepest)):
        for c in range(CHUNKS):
            after[c] = jnp.concatenate([after[c], exchange(after[c], level)], axis=0)
    sums = partials(1, [(value, swap(value)) for value in after])
    for level in range(deepest):
        sums = [next_step(value, level) for value in sums]
    ours = jnp.stack([add(value[0], own[0]) for value, own in zip(sums, own_after)], axis=1)
    theirs = jnp.stack([value[1] for value in sums], axis=1)

    def of_micro(value, mine):
        value = value.reshape(micro, rows, CHUNKS, width)
        return jnp.where(first == mine, value[0], value[1])

    keep = of_micro(ours, True)
    near = cross(of_micro(ours, False).astype(jnp.bfloat16), False, 1)
    far_same = cross(of_micro(theirs, True), True, 0)
    far_other = cross(of_micro(theirs, False), True, 1)
    same = (keep + far_same.astype(jnp.float32)).astype(jnp.bfloat16)
    other = add(near, far_other).astype(jnp.bfloat16)
    both = jnp.where(first, jnp.stack([same, other], axis=2), jnp.stack([other, same], axis=2))
    return both.reshape(1, rows, model_width)


def solution(mesh):
    placed = (
        P(None, ("groups", "expert"), None),
        P("section", None, ("groups", "expert"), None),
        P("section", None),
        P("section", None, None),
        P("section", None, "expert"),
        P("section", None, "expert"),
        P("section", "expert", None),
    )
    return jax.shard_map(
        local,
        mesh=mesh,
        in_specs=placed,
        out_specs=P("section", ("groups", "expert"), None),
        check_vma=False,
    )
```

```python
import functools

import jax
import jax.numpy as jnp
from jax import lax
from jax.experimental import pallas as pl
from jax.experimental.pallas import tpu as pltpu
from jax.sharding import PartitionSpec as P

FF = 1024
EXPERTS = 16
EPSILON = 1e-06
CHUNKS = 2
LANES = 128
SLOTS = 6
RESIDENT = 6
FETCHES = (2, 2, 2)
TOP = 59 << 20
IN_VMEM = pl.BlockSpec(memory_space=pltpu.VMEM)
ANYWHERE = pl.BlockSpec(memory_space=pl.ANY)


def bit_orders(count):
    bits = [1 << k for k in range(count.bit_length() - 1)]
    return bits, bits[1:2] + bits[:1] + bits[2:]


def block_of(order):
    table = [0]
    for bit in reversed(order):
        table = table + [b ^ bit for b in table]
    return table


def swap_tables(count):
    first, second = (block_of(order) for order in bit_orders(count))
    return [second.index(b) for b in first], [first.index(b) for b in second]


def exchange(value, level):
    count = lax.axis_size("expert")
    orders = bit_orders(count)
    pairs = [
        (2 * e + s, 2 * (e ^ orders[s][level]) + s) for e in range(count) for s in range(2)
    ]
    return lax.ppermute(value, ("expert", "section"), pairs)


def swap(value):
    return lax.ppermute(value, "section", [(0, 1), (1, 0)])


def add(left, right):
    return left.astype(jnp.float32) + right.astype(jnp.float32)


def next_step(value, level):
    half = value.shape[0] // 2
    received = exchange(value[half:], level)
    return add(value[:half], received).astype(jnp.bfloat16)


def cross(value, flip, to_other):
    count = lax.axis_size("expert")
    bit = bit_orders(count)[0][-1] if flip else 0
    pairs = [(2 * e + s, 2 * (e ^ bit) + (s ^ to_other)) for e in range(count) for s in range(2)]
    return lax.ppermute(value, ("expert", "section"), pairs)


def after_token(value, token):
    return value + token[None]


class Arena:
    def __init__(self, weights, width, slots, resident, top):
        self.resident = resident
        self.weights, self.width, self.slots = weights, width, slots
        self.units = weights[0].shape[2]
        self.blocks = weights[0].shape[1] // width
        self.tile = min(256, self.units)
        self.loads = 3 * self.blocks
        self.slot_rows = width * self.units // self.tile
        self.nbytes = slots * self.slot_rows * self.tile * 2
        self.limit = top - self.nbytes
        self.type = pltpu.VMEM((slots * self.slot_rows, self.tile), weights[0].dtype)

    def at(self, load):
        return load % self.slots * self.slot_rows

    def down_load(self, block):
        return 2 * self.blocks + block

    def copies(self, load, sources, arena, sems):
        made = []
        if load < 2 * self.blocks:
            source, block, depth = sources[load % 2], load // 2, self.width
            corners = [(block * depth, t * self.tile) for t in range(self.units // self.tile)]
        else:
            source, block, depth = sources[2], load - 2 * self.blocks, self.units
            corners = [(0, block * self.width + t * self.tile) for t in range(self.width // self.tile)]
        for t, (row, column) in enumerate(corners):
            made.append(
                pltpu.make_async_copy(
                    source.at[0, pl.ds(row, depth), pl.ds(column, self.tile)],
                    arena.at[pl.ds(self.at(load) + t * depth, depth)],
                    sems.at[t],
                )
            )
        return made


def call(body, layer, place, arena, inputs, outputs, scratch, loads, name, after=None, token=None, zeros=False, specs=None):
    n_in, n_out = len(inputs), len(outputs)
    extra = [] if after is None else [after]
    held = [] if arena is None else [arena]
    most = max(place.units, place.width) // place.tile

    def kernel(*refs):
        refs = list(refs)
        ins, refs = refs[:n_in], refs[n_in:]
        sources, refs = refs[:3], refs[3 + len(extra) + len(held) :]
        outs, refs = refs[:n_out], refs[n_out:]
        memory, refs = refs[0], refs[1:]
        if token is not None:
            marker, refs = refs[0], refs[1:]
            marker[...] = jnp.zeros_like(marker)
        sems, refs = refs[0], refs[1:]
        flying = {}

        def start(load):
            flying[load] = place.copies(load, sources, memory, sems.at[loads.index(load)])
            for copy in flying[load]:
                copy.start()

        def wait(load):
            for copy in flying.pop(load, []):
                copy.wait()

        def work():
            body(ins, outs, refs, memory, start, wait)
            for load in list(flying):
                wait(load)

        if layer is None:
            work()
        else:
            here = lax.axis_index("section") == layer
            pl.when(here)(work)
            if zeros:

                @pl.when(jnp.logical_not(here))
                def _():
                    for out in outs:
                        out[...] = jnp.zeros_like(out)

    shapes = list(outputs) + [place.type]
    if token is not None:
        shapes.append(pltpu.VMEM(token, jnp.bfloat16))
    moved = max(len(loads), 1) * place.slot_rows * place.tile * 2
    results = pl.pallas_call(
        kernel,
        in_specs=(specs or [IN_VMEM] * n_in) + [ANYWHERE] * (3 + len(extra)) + [IN_VMEM] * len(held),
        out_specs=[IN_VMEM] * len(shapes),
        out_shape=shapes,
        input_output_aliases={n_in + 3 + len(extra): n_out} if held else {},
        scratch_shapes=[pltpu.SemaphoreType.DMA((max(len(loads), 1), most))] + list(scratch),
        compiler_params=pltpu.CompilerParams(vmem_limit_bytes=place.limit),
        cost_estimate=pl.CostEstimate(flops=0, transcendentals=0, bytes_accessed=moved),
        name=name,
    )(*inputs, *place.weights, *extra, *held)
    return list(results)


def prepare(tokens, routes, width):
    micro, rows, _ = tokens.shape
    top = routes.shape[2]
    block = micro * rows

    def kernel(tokens_ref, routes_ref, out):
        section = lax.axis_index("section")
        for c in range(CHUNKS):
            at = pl.multiple_of((2 * c + section) * width, LANES)
            both = [tokens_ref[m, :, pl.ds(at, width)].astype(jnp.float32) for m in range(micro)]
            out[0, :, c * width : (c + 1) * width] = jnp.concatenate(both, 0).astype(jnp.bfloat16)
        lane = lax.broadcasted_iota(jnp.int32, (rows, LANES), 1)
        eye = lax.broadcasted_iota(jnp.int32, (rows, rows), 0) == lax.broadcasted_iota(
            jnp.int32, (rows, rows), 1
        )
        named = []
        for m in range(micro):
            value = jnp.zeros((rows, LANES), jnp.float32)
            for k in range(top):
                line = jnp.broadcast_to(routes_ref[0, m, k : k + 1].astype(jnp.float32), (rows, rows))
                column = jnp.sum(jnp.where(eye, line, 0.0), axis=1, keepdims=True)
                value = jnp.where(lane == k, column, value)
            named.append(value)
        out[0, :, CHUNKS * width :] = jnp.concatenate(named, 0).astype(jnp.bfloat16)

    return pl.pallas_call(
        kernel,
        in_specs=[IN_VMEM] * 2,
        out_specs=IN_VMEM,
        out_shape=jax.ShapeDtypeStruct((1, block, CHUNKS * width + LANES), jnp.bfloat16),
        name="prepare",
    )(tokens, routes)


def layer_body(place, top, together, ins, outs, scratch, memory, start, wait):
    gain, router, named = ins[-3:]
    scaled, stats, gate_sum, up_sum, hidden, routes, sem = scratch
    count, rows, width = outs[0].shape
    tile, units, blocks = place.tile, place.units, place.blocks
    model_width = gain.shape[1]
    section = lax.axis_index("section")
    tables = swap_tables(count)
    lane = lax.broadcasted_iota(jnp.int32, (rows, LANES), 1)
    bring = pltpu.make_async_copy(named.at[:, :, pl.ds(CHUNKS * width, LANES)], routes, sem)
    bring.start()
    for load in range(place.resident, place.slots):
        start(load)

    def used(load):
        if load + place.slots < place.loads:
            start(load + place.slots)

    def block_for_other(p):
        return jnp.where(section == 0, tables[0][p], tables[1][p])

    def assemble(chunk):
        own, other = ins[:2] if together else ins[2 * chunk : 2 * chunk + 2]
        columns = slice(chunk * width, (chunk + 1) * width) if together else slice(0, width)
        mine_at = pl.multiple_of((2 * chunk + section) * width, LANES)
        theirs_at = pl.multiple_of((2 * chunk + 1 - section) * width, LANES)
        mine_gain = gain[:, pl.ds(mine_at, width)]
        theirs_gain = gain[:, pl.ds(theirs_at, width)]
        for p in range(count):
            at = pl.ds(p * rows, rows)
            mine = own[p, :, columns].astype(jnp.float32)
            theirs = other[block_for_other(p), :, columns].astype(jnp.float32)
            scaled[at, pl.ds(mine_at, width)] = (mine * mine_gain).astype(jnp.bfloat16)
            scaled[at, pl.ds(theirs_at, width)] = (theirs * theirs_gain).astype(jnp.bfloat16)
            square = jnp.sum(mine * mine + theirs * theirs, axis=-1, keepdims=True)
            square = jnp.where(lane == EXPERTS, square, 0.0)
            stats[at, :] = square if chunk == 0 else stats[at, :] + square

    def gates_of():
        stats[:, :EXPERTS] = lax.dot_general(
            scaled[...], router[0], (((1,), (1,)), ((), ())), preferred_element_type=jnp.float32
        )
        values = stats[...]
        lanes = lax.broadcasted_iota(jnp.int32, values.shape, 1)
        total = jnp.sum(jnp.where(lanes == EXPERTS, values, 0.0), axis=-1, keepdims=True)
        factor = lax.rsqrt(total / model_width + EPSILON)
        affinity = jax.nn.sigmoid(values * factor)
        bring.wait()
        experts = routes[...].astype(jnp.float32).reshape(values.shape)
        hit = jnp.zeros(values.shape, jnp.bool_)
        for k in range(top):
            hit = hit | (experts[:, k : k + 1] == lanes.astype(jnp.float32))
        picked = jnp.where(hit & (lanes < EXPERTS), affinity, 0.0)
        gates = picked / jnp.sum(picked, axis=-1, keepdims=True)
        return factor, gates

    unit_at = lax.axis_index("expert") * units
    if not together:
        for chunk in range(CHUNKS):
            assemble(chunk)
        factor, gates = gates_of()
    for block in range(blocks):
        if together and block % 2 == 0:
            assemble(block // 2)
        if together and block == blocks - 1:
            factor, gates = gates_of()
        value = scaled.at[:, block * width : (block + 1) * width]
        for side, sums in enumerate((gate_sum, up_sum)):
            load = 2 * block + side
            wait(load)
            for t in range(units // tile):
                at = slice(t * tile, (t + 1) * tile)
                part = jnp.dot(
                    value[...],
                    memory[pl.ds(place.at(load) + t * width, width)],
                    preferred_element_type=jnp.float32,
                )
                if block > 0:
                    part += sums[:, at]
                if block < blocks - 1 or side == 0:
                    sums[:, at] = part
                    continue
                expert = (unit_at + t * tile) // FF
                lanes = lax.broadcasted_iota(jnp.int32, gates.shape, 1)
                weight = jnp.sum(jnp.where(lanes == expert, gates, 0.0), axis=-1, keepdims=True)
                gated = jax.nn.silu(gate_sum[:, at] * factor) * (part * (factor * weight))
                hidden[:, at] = gated.astype(jnp.bfloat16)
            used(load)

    for chunk in range(CHUNKS):
        places = []
        for side in range(2):
            load = place.down_load(2 * chunk + side)
            wait(load)
            places.append(place.at(load))
        for own in range(2):
            out = outs[2 * chunk + own]
            side = section if own else 1 - section
            base = jnp.where(side == 0, places[0], places[1])
            for t in range(width // tile):
                at = pl.multiple_of(base + t * units, 16)
                part = jnp.dot(
                    hidden[...], memory[pl.ds(at, units)], preferred_element_type=jnp.float32
                ).astype(jnp.bfloat16)
                to = slice(t * tile, (t + 1) * tile)
                for p in range(count):
                    out[p if own else block_for_other(p), :, to] = part[p * rows : (p + 1) * rows]
        for side in range(2):
            used(place.down_load(2 * chunk + side))


def run_layer(layer, place, arena, pairs, gain, router, named, top):
    count, rows, _ = pairs[0][0].shape
    total = count * rows
    shape = pltpu.VMEM((count, rows, place.width), jnp.bfloat16)
    scratch = [
        pltpu.VMEM((total, gain.shape[1]), jnp.bfloat16),
        pltpu.VMEM((total, LANES), jnp.float32),
        pltpu.VMEM((total, place.units), jnp.float32),
        pltpu.VMEM((total, place.units), jnp.float32),
        pltpu.VMEM((total, place.units), jnp.bfloat16),
        pltpu.VMEM((count, rows, LANES), jnp.bfloat16),
        pltpu.SemaphoreType.DMA,
    ]
    inputs = [
        pltpu.with_memory_space_constraint(value, pltpu.VMEM) for pair in pairs for value in pair
    ] + [gain, router, named]
    specs = [IN_VMEM] * (len(inputs) - 1) + [ANYWHERE]
    results = call(
        functools.partial(layer_body, place, top, len(pairs) == 1),
        layer, place, arena, inputs, [shape] * (2 * CHUNKS), scratch,
        list(range(place.resident, place.loads)), "layer", zeros=True, specs=specs,
    )
    return results[:-1], results[-1]


def run_layer_plainly(layer, weights, pairs, gain, router, named, top):
    count, rows, _ = pairs[0][0].shape
    model_width = gain.shape[1]
    width = model_width // (2 * CHUNKS)
    units = weights[0].shape[2]
    first = lax.axis_index("section") == 0
    tables = jnp.array(swap_tables(count), jnp.int32)
    table = jnp.where(first, tables[0], tables[1])
    back = jnp.where(first, tables[1], tables[0])
    columns = []
    if len(pairs) == 1:
        pairs = [
            [side[:, :, c * width : (c + 1) * width] for side in pairs[0]] for c in range(CHUNKS)
        ]
    for own, other in pairs:
        other = other[table]
        columns += [jnp.where(first, own, other), jnp.where(first, other, own)]
    values = jnp.concatenate(columns, axis=-1).reshape(count * rows, model_width).astype(jnp.float32)
    factor = lax.rsqrt(jnp.mean(values * values, axis=-1, keepdims=True) + EPSILON)
    scaled = (values * gain).astype(jnp.bfloat16)

    def product(left, right):
        return jnp.dot(left, right, preferred_element_type=jnp.float32)

    affinity = jax.nn.sigmoid(product(scaled, router[0].T) * factor)
    experts = named[:, :, CHUNKS * width : CHUNKS * width + top].reshape(count * rows, top).astype(jnp.int32)
    hit = jnp.any(experts[:, :, None] == jnp.arange(EXPERTS, dtype=jnp.int32), axis=1)
    picked = jnp.where(hit, affinity, 0.0)
    gates = picked / jnp.sum(picked, axis=-1, keepdims=True)
    of_unit = (lax.axis_index("expert") * units + jnp.arange(units, dtype=jnp.int32)) // FF
    weight = jnp.take(gates, of_unit, axis=1)
    up_part = product(scaled, weights[1][0]) * (factor * weight)
    hidden = (jax.nn.silu(product(scaled, weights[0][0]) * factor) * up_part).astype(jnp.bfloat16)
    out = product(hidden, weights[2][0]).astype(jnp.bfloat16)
    out = out.reshape(count, rows, CHUNKS, 2, width)
    out = jnp.where(lax.axis_index("section") == layer, out, jnp.zeros_like(out))
    parts = []
    for c in range(CHUNKS):
        left, right = out[:, :, c, 0], out[:, :, c, 1]
        parts += [jnp.where(first, right, left)[back], jnp.where(first, left, right)]
    return parts


def fetch(place, arena, loads, after, token):
    def body(ins, outs, scratch, memory, start, wait):
        for load in loads:
            start(load)

    return call(body, None, place, arena, [], [], [], loads, "fetch", after=after, token=token)


def local(tokens, routes, norm_gain, router_weight, gate_weight, up_weight, down_weight):
    count = lax.axis_size("expert")
    micro, rows, model_width = tokens.shape
    width = model_width // (2 * CHUNKS)
    top = routes.shape[-1]
    section = lax.axis_index("section")
    first = section == 0
    deepest = count.bit_length() - 2
    router = jnp.swapaxes(router_weight, 1, 2)
    weights = (gate_weight, up_weight, down_weight)
    held = count * micro * rows <= 2 * LANES
    place = Arena(weights, width, SLOTS, RESIDENT, TOP)

    def partials(layer, pairs):
        nonlocal arena
        if held:
            parts, arena = run_layer(layer, place, arena, pairs, norm_gain, router, named, top)
        else:
            parts = run_layer_plainly(layer, weights, pairs, norm_gain, router, named, top)
        moved = [swap(parts[2 * c]) for c in range(CHUNKS)]
        return [add(parts[2 * c + 1], moved[c]).astype(jnp.bfloat16) for c in range(CHUNKS)]

    gathered = prepare(tokens, jnp.swapaxes(routes, 2, 3), width)
    arena = None
    loads = list(range(RESIDENT))
    fetches = FETCHES
    for level in reversed(range(deepest + 1)):
        received = exchange(gathered, level)
        if held and fetches:
            todo, loads, fetches = loads[: fetches[0]], loads[fetches[0] :], fetches[1:]
            arena, token = fetch(place, arena, todo, gathered, received.shape[1:])
            received = after_token(received, token)
        gathered = jnp.concatenate([gathered, received], axis=0)
    if held and loads:
        arena, _ = fetch(place, arena, loads, gathered, (8, LANES))
    named = gathered
    moved = partials(0, [(gathered, swap(gathered))])

    after = list(moved)
    for level in range(deepest):
        after = [next_step(value, level) for value in after]
    for c in range(CHUNKS):
        value = add(after[c], jnp.flip(exchange(after[c], deepest), axis=0))
        residual = gathered[:2, :, c * width : (c + 1) * width].astype(jnp.float32)
        after[c] = (residual + value).astype(jnp.bfloat16)
    own_after = [value[:1] for value in after]
    for level in reversed(range(deepest)):
        for c in range(CHUNKS):
            after[c] = jnp.concatenate([after[c], exchange(after[c], level)], axis=0)
    sums = partials(1, [(value, swap(value)) for value in after])
    for level in range(deepest):
        sums = [next_step(value, level) for value in sums]
    ours = jnp.stack([add(value[0], own[0]) for value, own in zip(sums, own_after)], axis=1)
    theirs = jnp.stack([value[1] for value in sums], axis=1)

    def of_micro(value, mine):
        value = value.reshape(micro, rows, CHUNKS, width)
        return jnp.where(first == mine, value[0], value[1])

    keep = of_micro(ours, True)
    near = cross(of_micro(ours, False).astype(jnp.bfloat16), False, 1)
    far_same = cross(of_micro(theirs, True), True, 0)
    far_other = cross(of_micro(theirs, False), True, 1)
    same = (keep + far_same.astype(jnp.float32)).astype(jnp.bfloat16)
    other = add(near, far_other).astype(jnp.bfloat16)
    both = jnp.where(first, jnp.stack([same, other], axis=2), jnp.stack([other, same], axis=2))
    return both.reshape(1, rows, model_width)


def solution(mesh):
    placed = (
        P(None, ("groups", "expert"), None),
        P("section", None, ("groups", "expert"), None),
        P("section", None),
        P("section", None, None),
        P("section", None, "expert"),
        P("section", None, "expert"),
        P("section", "expert", None),
    )
    return jax.shard_map(
        local,
        mesh=mesh,
        in_specs=placed,
        out_specs=P("section", ("groups", "expert"), None),
        check_vma=False,
    )
```

```python
import functools

import jax
import jax.numpy as jnp
from jax import lax
from jax.experimental import pallas as pl
from jax.experimental.pallas import tpu as pltpu
from jax.sharding import PartitionSpec as P

FF = 1024
EXPERTS = 16
EPSILON = 1e-06
CHUNKS = 2
LANES = 128
SLOTS = 6
RESIDENT = 6
FETCHES = (2, 2, 2)
TOP = 59 << 20
IN_VMEM = pl.BlockSpec(memory_space=pltpu.VMEM)
ANYWHERE = pl.BlockSpec(memory_space=pl.ANY)


def bit_orders(count):
    bits = [1 << k for k in range(count.bit_length() - 1)]
    return bits, bits[1:2] + bits[:1] + bits[2:]


def block_of(order):
    table = [0]
    for bit in reversed(order):
        table = table + [b ^ bit for b in table]
    return table


def swap_tables(count):
    first, second = (block_of(order) for order in bit_orders(count))
    return [second.index(b) for b in first], [first.index(b) for b in second]


def exchange(value, level):
    count = lax.axis_size("expert")
    orders = bit_orders(count)
    pairs = [
        (2 * e + s, 2 * (e ^ orders[s][level]) + s) for e in range(count) for s in range(2)
    ]
    return lax.ppermute(value, ("expert", "section"), pairs)


def swap(value):
    return lax.ppermute(value, "section", [(0, 1), (1, 0)])


def add(left, right):
    return left.astype(jnp.float32) + right.astype(jnp.float32)


def next_step(value, level):
    half = value.shape[0] // 2
    received = exchange(value[half:], level)
    return add(value[:half], received).astype(jnp.bfloat16)


def cross(value, flip, to_other):
    count = lax.axis_size("expert")
    bit = bit_orders(count)[0][-1] if flip else 0
    pairs = [(2 * e + s, 2 * (e ^ bit) + (s ^ to_other)) for e in range(count) for s in range(2)]
    return lax.ppermute(value, ("expert", "section"), pairs)


def after_token(value, token):
    return value + token[None]


class Arena:
    def __init__(self, weights, width, slots, resident, top):
        self.resident = resident
        self.weights, self.width, self.slots = weights, width, slots
        self.units = weights[0].shape[2]
        self.blocks = weights[0].shape[1] // width
        self.tile = min(256, self.units)
        self.loads = 3 * self.blocks
        self.slot_rows = width * self.units // self.tile
        self.nbytes = slots * self.slot_rows * self.tile * 2
        self.limit = top - self.nbytes
        self.type = pltpu.VMEM((slots * self.slot_rows, self.tile), weights[0].dtype)

    def at(self, load):
        return load % self.slots * self.slot_rows

    def down_load(self, block):
        return 2 * self.blocks + block

    def copies(self, load, sources, arena, sems):
        made = []
        if load < 2 * self.blocks:
            source, block, depth = sources[load % 2], load // 2, self.width
            corners = [(block * depth, t * self.tile) for t in range(self.units // self.tile)]
        else:
            source, block, depth = sources[2], load - 2 * self.blocks, self.units
            corners = [(0, block * self.width + t * self.tile) for t in range(self.width // self.tile)]
        for t, (row, column) in enumerate(corners):
            made.append(
                pltpu.make_async_copy(
                    source.at[0, pl.ds(row, depth), pl.ds(column, self.tile)],
                    arena.at[pl.ds(self.at(load) + t * depth, depth)],
                    sems.at[t],
                )
            )
        return made


def call(body, layer, place, arena, inputs, outputs, scratch, loads, name, after=None, token=None, zeros=False, specs=None):
    n_in, n_out = len(inputs), len(outputs)
    extra = [] if after is None else [after]
    held = [] if arena is None else [arena]
    most = max(place.units, place.width) // place.tile

    def kernel(*refs):
        refs = list(refs)
        ins, refs = refs[:n_in], refs[n_in:]
        sources, refs = refs[:3], refs[3 + len(extra) + len(held) :]
        outs, refs = refs[:n_out], refs[n_out:]
        memory, refs = refs[0], refs[1:]
        if token is not None:
            marker, refs = refs[0], refs[1:]
            marker[...] = jnp.zeros_like(marker)
        sems, refs = refs[0], refs[1:]
        flying = {}

        def start(load):
            flying[load] = place.copies(load, sources, memory, sems.at[loads.index(load)])
            for copy in flying[load]:
                copy.start()

        def wait(load):
            for copy in flying.pop(load, []):
                copy.wait()

        def work():
            body(ins, outs, refs, memory, start, wait)
            for load in list(flying):
                wait(load)

        if layer is None:
            work()
        else:
            here = lax.axis_index("section") == layer
            pl.when(here)(work)
            if zeros:

                @pl.when(jnp.logical_not(here))
                def _():
                    for out in outs:
                        out[...] = jnp.zeros_like(out)

    shapes = list(outputs) + [place.type]
    if token is not None:
        shapes.append(pltpu.VMEM(token, jnp.bfloat16))
    moved = max(len(loads), 1) * place.slot_rows * place.tile * 2
    results = pl.pallas_call(
        kernel,
        in_specs=(specs or [IN_VMEM] * n_in) + [ANYWHERE] * (3 + len(extra)) + [IN_VMEM] * len(held),
        out_specs=[IN_VMEM] * len(shapes),
        out_shape=shapes,
        input_output_aliases={n_in + 3 + len(extra): n_out} if held else {},
        scratch_shapes=[pltpu.SemaphoreType.DMA((max(len(loads), 1), most))] + list(scratch),
        compiler_params=pltpu.CompilerParams(vmem_limit_bytes=place.limit),
        cost_estimate=pl.CostEstimate(flops=0, transcendentals=0, bytes_accessed=moved),
        name=name,
    )(*inputs, *place.weights, *extra, *held)
    return list(results)


def prepare(tokens, routes, width):
    micro, rows, _ = tokens.shape
    top = routes.shape[2]
    block = micro * rows

    def kernel(tokens_ref, routes_ref, out):
        section = lax.axis_index("section")
        for c in range(CHUNKS):
            at = pl.multiple_of((2 * c + section) * width, LANES)
            both = [tokens_ref[m, :, pl.ds(at, width)].astype(jnp.float32) for m in range(micro)]
            out[0, :, c * width : (c + 1) * width] = jnp.concatenate(both, 0).astype(jnp.bfloat16)
        lane = lax.broadcasted_iota(jnp.int32, (rows, LANES), 1)
        eye = lax.broadcasted_iota(jnp.int32, (rows, rows), 0) == lax.broadcasted_iota(
            jnp.int32, (rows, rows), 1
        )
        named = []
        for m in range(micro):
            value = jnp.zeros((rows, LANES), jnp.float32)
            for k in range(top):
                line = jnp.broadcast_to(routes_ref[0, m, k : k + 1].astype(jnp.float32), (rows, rows))
                column = jnp.sum(jnp.where(eye, line, 0.0), axis=1, keepdims=True)
                value = jnp.where(lane == k, column, value)
            named.append(value)
        out[0, :, CHUNKS * width :] = jnp.concatenate(named, 0).astype(jnp.bfloat16)

    return pl.pallas_call(
        kernel,
        in_specs=[IN_VMEM] * 2,
        out_specs=IN_VMEM,
        out_shape=jax.ShapeDtypeStruct((1, block, CHUNKS * width + LANES), jnp.bfloat16),
        name="prepare",
    )(tokens, routes)


def layer_body(place, top, together, ins, outs, scratch, memory, start, wait):
    gain, router, named = ins[-3:]
    scaled, stats, gate_sum, up_sum, hidden, routes, sem = scratch
    count, rows, width = outs[0].shape
    tile, units, blocks = place.tile, place.units, place.blocks
    model_width = gain.shape[1]
    section = lax.axis_index("section")
    tables = swap_tables(count)
    lane = lax.broadcasted_iota(jnp.int32, (rows, LANES), 1)
    bring = pltpu.make_async_copy(named.at[:, :, pl.ds(CHUNKS * width, LANES)], routes, sem)
    bring.start()
    for load in range(place.resident, place.slots):
        start(load)

    def used(load):
        if load + place.slots < place.loads:
            start(load + place.slots)

    def block_for_other(p):
        return jnp.where(section == 0, tables[0][p], tables[1][p])

    def assemble(chunk):
        own, other = ins[:2] if together else ins[2 * chunk : 2 * chunk + 2]
        columns = slice(chunk * width, (chunk + 1) * width) if together else slice(0, width)
        mine_at = pl.multiple_of((2 * chunk + section) * width, LANES)
        theirs_at = pl.multiple_of((2 * chunk + 1 - section) * width, LANES)
        mine_gain = gain[:, pl.ds(mine_at, width)]
        theirs_gain = gain[:, pl.ds(theirs_at, width)]
        for p in range(count):
            at = pl.ds(p * rows, rows)
            mine = own[p, :, columns].astype(jnp.float32)
            theirs = other[block_for_other(p), :, columns].astype(jnp.float32)
            scaled[at, pl.ds(mine_at, width)] = (mine * mine_gain).astype(jnp.bfloat16)
            scaled[at, pl.ds(theirs_at, width)] = (theirs * theirs_gain).astype(jnp.bfloat16)
            square = jnp.sum(mine * mine + theirs * theirs, axis=-1, keepdims=True)
            square = jnp.where(lane == EXPERTS, square, 0.0)
            stats[at, :] = square if chunk == 0 else stats[at, :] + square

    def gates_of():
        stats[:, :EXPERTS] = lax.dot_general(
            scaled[...], router[0], (((1,), (1,)), ((), ())), preferred_element_type=jnp.float32
        )
        values = stats[...]
        lanes = lax.broadcasted_iota(jnp.int32, values.shape, 1)
        total = jnp.sum(jnp.where(lanes == EXPERTS, values, 0.0), axis=-1, keepdims=True)
        factor = lax.rsqrt(total / model_width + EPSILON)
        affinity = jax.nn.sigmoid(values * factor)
        bring.wait()
        experts = routes[...].astype(jnp.float32).reshape(values.shape)
        hit = jnp.zeros(values.shape, jnp.bool_)
        for k in range(top):
            hit = hit | (experts[:, k : k + 1] == lanes.astype(jnp.float32))
        picked = jnp.where(hit & (lanes < EXPERTS), affinity, 0.0)
        gates = picked / jnp.sum(picked, axis=-1, keepdims=True)
        return factor, gates

    unit_at = lax.axis_index("expert") * units
    for block in range(blocks):
        if block == 0:
            assemble(0)
        if block == 1:
            for chunk in range(1, CHUNKS):
                assemble(chunk)
            factor, gates = gates_of()
        value = scaled.at[:, block * width : (block + 1) * width]
        for side, sums in enumerate((gate_sum, up_sum)):
            load = 2 * block + side
            wait(load)
            for t in range(units // tile):
                at = slice(t * tile, (t + 1) * tile)
                part = jnp.dot(
                    value[...],
                    memory[pl.ds(place.at(load) + t * width, width)],
                    preferred_element_type=jnp.float32,
                )
                if block > 0:
                    part += sums[:, at]
                if block < blocks - 1 or side == 0:
                    sums[:, at] = part
                    continue
                expert = (unit_at + t * tile) // FF
                lanes = lax.broadcasted_iota(jnp.int32, gates.shape, 1)
                weight = jnp.sum(jnp.where(lanes == expert, gates, 0.0), axis=-1, keepdims=True)
                gated = jax.nn.silu(gate_sum[:, at] * factor) * (part * (factor * weight))
                hidden[:, at] = gated.astype(jnp.bfloat16)
            used(load)

    for chunk in range(CHUNKS):
        places = []
        for side in range(2):
            load = place.down_load(2 * chunk + side)
            wait(load)
            places.append(place.at(load))
        for own in range(2):
            out = outs[2 * chunk + own]
            side = section if own else 1 - section
            base = jnp.where(side == 0, places[0], places[1])
            for t in range(width // tile):
                at = pl.multiple_of(base + t * units, 16)
                part = jnp.dot(
                    hidden[...], memory[pl.ds(at, units)], preferred_element_type=jnp.float32
                ).astype(jnp.bfloat16)
                to = slice(t * tile, (t + 1) * tile)
                for p in range(count):
                    out[p if own else block_for_other(p), :, to] = part[p * rows : (p + 1) * rows]
        for side in range(2):
            used(place.down_load(2 * chunk + side))


def run_layer(layer, place, arena, pairs, gain, router, named, top):
    count, rows, _ = pairs[0][0].shape
    total = count * rows
    shape = pltpu.VMEM((count, rows, place.width), jnp.bfloat16)
    scratch = [
        pltpu.VMEM((total, gain.shape[1]), jnp.bfloat16),
        pltpu.VMEM((total, LANES), jnp.float32),
        pltpu.VMEM((total, place.units), jnp.float32),
        pltpu.VMEM((total, place.units), jnp.float32),
        pltpu.VMEM((total, place.units), jnp.bfloat16),
        pltpu.VMEM((count, rows, LANES), jnp.bfloat16),
        pltpu.SemaphoreType.DMA,
    ]
    inputs = [
        pltpu.with_memory_space_constraint(value, pltpu.VMEM) for pair in pairs for value in pair
    ] + [gain, router, named]
    specs = [IN_VMEM] * (len(inputs) - 1) + [ANYWHERE]
    results = call(
        functools.partial(layer_body, place, top, len(pairs) == 1),
        layer, place, arena, inputs, [shape] * (2 * CHUNKS), scratch,
        list(range(place.resident, place.loads)), "layer", zeros=True, specs=specs,
    )
    return results[:-1], results[-1]


def run_layer_plainly(layer, weights, pairs, gain, router, named, top):
    count, rows, _ = pairs[0][0].shape
    model_width = gain.shape[1]
    width = model_width // (2 * CHUNKS)
    units = weights[0].shape[2]
    first = lax.axis_index("section") == 0
    tables = jnp.array(swap_tables(count), jnp.int32)
    table = jnp.where(first, tables[0], tables[1])
    back = jnp.where(first, tables[1], tables[0])
    columns = []
    if len(pairs) == 1:
        pairs = [
            [side[:, :, c * width : (c + 1) * width] for side in pairs[0]] for c in range(CHUNKS)
        ]
    for own, other in pairs:
        other = other[table]
        columns += [jnp.where(first, own, other), jnp.where(first, other, own)]
    values = jnp.concatenate(columns, axis=-1).reshape(count * rows, model_width).astype(jnp.float32)
    factor = lax.rsqrt(jnp.mean(values * values, axis=-1, keepdims=True) + EPSILON)
    scaled = (values * gain).astype(jnp.bfloat16)

    def product(left, right):
        return jnp.dot(left, right, preferred_element_type=jnp.float32)

    affinity = jax.nn.sigmoid(product(scaled, router[0].T) * factor)
    experts = named[:, :, CHUNKS * width : CHUNKS * width + top].reshape(count * rows, top).astype(jnp.int32)
    hit = jnp.any(experts[:, :, None] == jnp.arange(EXPERTS, dtype=jnp.int32), axis=1)
    picked = jnp.where(hit, affinity, 0.0)
    gates = picked / jnp.sum(picked, axis=-1, keepdims=True)
    of_unit = (lax.axis_index("expert") * units + jnp.arange(units, dtype=jnp.int32)) // FF
    weight = jnp.take(gates, of_unit, axis=1)
    up_part = product(scaled, weights[1][0]) * (factor * weight)
    hidden = (jax.nn.silu(product(scaled, weights[0][0]) * factor) * up_part).astype(jnp.bfloat16)
    out = product(hidden, weights[2][0]).astype(jnp.bfloat16)
    out = out.reshape(count, rows, CHUNKS, 2, width)
    out = jnp.where(lax.axis_index("section") == layer, out, jnp.zeros_like(out))
    parts = []
    for c in range(CHUNKS):
        left, right = out[:, :, c, 0], out[:, :, c, 1]
        parts += [jnp.where(first, right, left)[back], jnp.where(first, left, right)]
    return parts


def fetch(place, arena, loads, after, token):
    def body(ins, outs, scratch, memory, start, wait):
        for load in loads:
            start(load)

    return call(body, None, place, arena, [], [], [], loads, "fetch", after=after, token=token)


def local(tokens, routes, norm_gain, router_weight, gate_weight, up_weight, down_weight):
    count = lax.axis_size("expert")
    micro, rows, model_width = tokens.shape
    width = model_width // (2 * CHUNKS)
    top = routes.shape[-1]
    section = lax.axis_index("section")
    first = section == 0
    deepest = count.bit_length() - 2
    router = jnp.swapaxes(router_weight, 1, 2)
    weights = (gate_weight, up_weight, down_weight)
    held = count * micro * rows <= 2 * LANES
    place = Arena(weights, width, SLOTS, RESIDENT, TOP)

    def partials(layer, pairs):
        nonlocal arena
        if held:
            parts, arena = run_layer(layer, place, arena, pairs, norm_gain, router, named, top)
        else:
            parts = run_layer_plainly(layer, weights, pairs, norm_gain, router, named, top)
        moved = [swap(parts[2 * c]) for c in range(CHUNKS)]
        return [add(parts[2 * c + 1], moved[c]).astype(jnp.bfloat16) for c in range(CHUNKS)]

    gathered = prepare(tokens, jnp.swapaxes(routes, 2, 3), width)
    arena = None
    loads = list(range(RESIDENT))
    fetches = FETCHES
    for level in reversed(range(deepest + 1)):
        received = exchange(gathered, level)
        if held and fetches:
            todo, loads, fetches = loads[: fetches[0]], loads[fetches[0] :], fetches[1:]
            arena, token = fetch(place, arena, todo, gathered, received.shape[1:])
            received = after_token(received, token)
        gathered = jnp.concatenate([gathered, received], axis=0)
    if held and loads:
        arena, _ = fetch(place, arena, loads, gathered, (8, LANES))
    named = gathered
    moved = partials(0, [(gathered, swap(gathered))])

    after = list(moved)
    for level in range(deepest):
        after = [next_step(value, level) for value in after]
    for c in range(CHUNKS):
        value = add(after[c], jnp.flip(exchange(after[c], deepest), axis=0))
        residual = gathered[:2, :, c * width : (c + 1) * width].astype(jnp.float32)
        after[c] = (residual + value).astype(jnp.bfloat16)
    own_after = [value[:1] for value in after]
    for level in reversed(range(deepest)):
        for c in range(CHUNKS):
            after[c] = jnp.concatenate([after[c], exchange(after[c], level)], axis=0)
    sums = partials(1, [(value, swap(value)) for value in after])
    for level in range(deepest):
        sums = [next_step(value, level) for value in sums]
    ours = jnp.stack([add(value[0], own[0]) for value, own in zip(sums, own_after)], axis=1)
    theirs = jnp.stack([value[1] for value in sums], axis=1)

    def of_micro(value, mine):
        value = value.reshape(micro, rows, CHUNKS, width)
        return jnp.where(first == mine, value[0], value[1])

    keep = of_micro(ours, True)
    near = cross(of_micro(ours, False).astype(jnp.bfloat16), False, 1)
    far_same = cross(of_micro(theirs, True), True, 0)
    far_other = cross(of_micro(theirs, False), True, 1)
    same = (keep + far_same.astype(jnp.float32)).astype(jnp.bfloat16)
    other = add(near, far_other).astype(jnp.bfloat16)
    both = jnp.where(first, jnp.stack([same, other], axis=2), jnp.stack([other, same], axis=2))
    return both.reshape(1, rows, model_width)


def solution(mesh):
    placed = (
        P(None, ("groups", "expert"), None),
        P("section", None, ("groups", "expert"), None),
        P("section", None),
        P("section", None, None),
        P("section", None, "expert"),
        P("section", None, "expert"),
        P("section", "expert", None),
    )
    return jax.shard_map(
        local,
        mesh=mesh,
        in_specs=placed,
        out_specs=P("section", ("groups", "expert"), None),
        check_vma=False,
    )
```
